256 devices in a mesh: fsdp: 32 (over z_hi, x, core), tp: 8 (over y, z_lo).
Axes of the slice: x: 4, y: 4, z: 8 (z_hi: 4, z_lo: 2; z = z_hi * 2 + z_lo), core: 2. Of those that a mesh axis runs over, the one named last changes fastest.
Arguments:
- activations: bfloat16 [8192, 8192], P('fsdp'), may hold values from -6 to 6
- grad_output: bfloat16 [8192, 28672], P('fsdp', 'tp'), may hold values from -0.1875 to 0.1875
- projector: bfloat16 [8192, 1024], P('fsdp'), may hold values from -0.125 to 0.125
- first_moment: float32 [1024, 28672], P('fsdp', 'tp'), may hold values from -0.625 to 0.625
- second_moment: float32 [1024, 28672], P('fsdp', 'tp'), may hold values from 0.01 to 0.5
Outputs:
- new_first: float32 [1024, 28672], P('fsdp', 'tp')
- new_second: float32 [1024, 28672], P('fsdp', 'tp')
- weight_update: bfloat16 [8192, 28672], P('fsdp', 'tp')
The draws below stay inside these ranges and needn't reach their ends.
All inputs are finite; a program needn't handle non-finite values.
Results may differ from the reference program's by a relative error of at most 0.0059.
Values may be sent and summed in bfloat16 or wider, within the bound.
No kernel may reach another device: no remote copies, remote signals or barrier semaphores. Data moves between devices by JAX's collectives and lax.ppermute only.
A program may use at most 64 MiB of HBM per device.

```python
import math
import jax
import jax.numpy as jnp

D = 8192
FF = 28672
R = 1024
TOKENS = 8192


def raised(array, rng, source, target, shards_of, factor):
    owner, partner = [(jnp.arange(array.shape[position]) // (array.shape[position] // shards_of)).reshape([-1 if axis == position else 1 for axis in range(array.ndim)]) for position in (source, target)]
    chosen = jax.random.permutation(rng, shards_of)[partner]
    strong = (owner == chosen) | (owner == (partner + shards_of // 2) % shards_of)
    return jnp.where(strong, factor * array, array)


def shard_levels(own_key, extent, shards, smallest, top_value):
    def one(position, parts):
        steps = jax.random.uniform(jax.random.fold_in(jax.random.fold_in(own_key, 6), position), (parts,), jnp.float32, smallest / len(shards), top_value / len(shards))
        return jnp.repeat(jnp.exp(steps), extent[position] // parts).reshape((-1,) + (1,) * (len(extent) - position - 1))

    factor_of = one(*shards[0])
    for cut in shards[1:]:
        factor_of = factor_of * one(*cut)
    return factor_of


def noise(rng, shape, spread, reach, split=(), kind=jnp.bfloat16):
    factor_of = shard_levels(rng, shape, split, -0.22, 0.18) if split else 1.0
    result = jax.random.normal(rng, shape, jnp.float32) * spread * factor_of
    return jnp.minimum(jnp.maximum(result, -reach), reach).astype(kind)


def heavy_noise(key, extent, spread, limit, split, heavy, dtype=jnp.bfloat16):
    values = spread * jax.random.normal(key, extent, jnp.float32)
    if split:
        values = values * shard_levels(key, extent, split, -0.22, 0.18)
    return jnp.clip(raised(values, jax.random.fold_in(key, 3), *heavy), -limit, limit).astype(dtype)


def setup_inputs(seed: int = 0) -> dict:
    keys = jax.random.split(jax.random.key(seed), 6)
    activations = noise(keys[0], (TOKENS, D), 1.0, 6.0, ((0, 32),))
    grad_output = noise(keys[1], (TOKENS, FF), (3 * TOKENS ** -0.5), 0.1875, ((0, 32), (1, 8)))
    projector = heavy_noise(keys[2], (D, R), D ** -0.5, 0.125, ((0, 32),), (0, 1, 32, 2.75))
    first_moment = noise(keys[3], (R, FF), 0.1, 0.625, ((0, 32), (1, 8)), jnp.float32)
    second_moment = jnp.clip(jnp.exp(math.log(0.5) - 3.912023 * jax.random.uniform(keys[4], (R, FF), jnp.float32) ** shard_levels(keys[4], (R, FF), ((0, 32), (1, 8)), -0.2, 0.2)), 0.01, 0.5)
    return {"activations": activations, "grad_output": grad_output, "projector": projector, "first_moment": first_moment, "second_moment": second_moment}


first_fix = 0.9999734386011124
second_fix = 0.6339676587267705

def reference(activations, grad_output, projector, first_moment, second_moment):
    coords = jnp.dot(activations, projector, preferred_element_type=jnp.float32).astype(jnp.bfloat16)
    lowrank = jnp.dot(coords.T, grad_output, preferred_element_type=jnp.float32)
    new_first = 0.9 * first_moment + 0.1 * lowrank
    new_second = 0.99 * second_moment + 0.01 * lowrank * lowrank
    direction = (new_first / first_fix / (jnp.sqrt(new_second / second_fix) + 1e-08)).astype(jnp.bfloat16)
    weight_update = jnp.dot(projector, direction, preferred_element_type=jnp.float32).astype(jnp.bfloat16)
    return (new_first, new_second, weight_update)
```

```python
import jax
import jax.numpy as jnp
from jax import lax
from jax.sharding import PartitionSpec as P

first_fix = 0.9999734386011124
second_fix = 0.6339676587267705


def body(activations, grad_output, projector, first_moment, second_moment):
    rank_width = projector.shape[1]
    tp_count = lax.axis_size("tp")
    tp_place = lax.axis_index("tp")
    column_count = rank_width // tp_count
    proj_block = lax.dynamic_slice_in_dim(projector, tp_place * column_count, column_count, 1)
    proj_columns = lax.all_gather(proj_block, "fsdp", axis=0, tiled=True)
    own_coords = jnp.dot(
        activations, proj_columns, preferred_element_type=jnp.float32
    ).astype(jnp.bfloat16)
    coords = lax.all_gather(own_coords, "tp", axis=1, tiled=True)
    partial = lax.dot_general(
        coords, grad_output, (((0,), (0,)), ((), ())), preferred_element_type=jnp.float32
    ).astype(jnp.bfloat16)
    lowrank = lax.psum_scatter(partial, "fsdp", scatter_dimension=0, tiled=True).astype(
        jnp.float32
    )
    new_first = 0.9 * first_moment + 0.1 * lowrank
    new_second = 0.99 * second_moment + 0.01 * lowrank * lowrank
    direction = (new_first / first_fix / (jnp.sqrt(new_second / second_fix) + 1e-08)).astype(
        jnp.bfloat16
    )
    summed = jnp.dot(
        projector,
        lax.all_gather(direction, "fsdp", axis=0, tiled=True),
        preferred_element_type=jnp.float32,
    )
    return (new_first, new_second, summed.astype(jnp.bfloat16))


def solution(mesh):
    return jax.shard_map(
        body,
        mesh=mesh,
        in_specs=(
            P("fsdp", None),
            P("fsdp", "tp"),
            P("fsdp", None),
            P("fsdp", "tp"),
            P("fsdp", "tp"),
        ),
        out_specs=(P("fsdp", "tp"), P("fsdp", "tp"), P("fsdp", "tp")),
        check_vma=False,
    )
```

```python
import functools

import jax
import jax.numpy as jnp
from jax import lax
from jax.experimental import pallas as pl
from jax.experimental.pallas import tpu as pltpu
from jax.sharding import PartitionSpec as P

first_fix = 0.9999734386011124
second_fix = 0.6339676587267705
BF = jnp.bfloat16
F32 = jnp.float32


def swap(array, axis, mask):
    count = lax.axis_size(axis)
    return lax.ppermute(array, axis, [(i, i ^ mask) for i in range(count)])


def doubled(masks):
    order = [0]
    for mask in masks:
        order = order + [o ^ mask for o in order]
    return order


def gather(array, axis, masks):
    for mask in masks:
        array = jnp.concatenate([array, swap(array, axis, mask)], axis=0)
    return array


def by_core(core, own, other, axis):
    return jnp.where(
        core == 0,
        jnp.concatenate([own, other], axis=axis),
        jnp.concatenate([other, own], axis=axis),
    )


def one_hot(rows, columns):
    return (rows[:, None] == columns[None, :]).astype(BF)


def expand(blocks, width):
    return (blocks[:, None] * width + jnp.arange(width, dtype=jnp.int32)[None, :]).reshape(-1)


def table(order):
    return jnp.array(order, dtype=jnp.int32)


def reorder_kernel(width, index_ref, in_ref, out_ref):
    for k in range(out_ref.shape[1] // width):
        start = pl.multiple_of(index_ref[k] * width, width)
        out_ref[:, k * width : (k + 1) * width] = in_ref[:, pl.ds(start, width)]


def reorder(array, index, width):

    return pl.pallas_call(
        functools.partial(reorder_kernel, width),
        out_shape=jax.ShapeDtypeStruct(array.shape, array.dtype),
        in_specs=[
            pl.BlockSpec(memory_space=pltpu.SMEM),
            pl.BlockSpec(memory_space=pltpu.VMEM),
        ],
        out_specs=pl.BlockSpec(memory_space=pltpu.VMEM),
        compiler_params=pltpu.CompilerParams(vmem_limit_bytes=24 * 2**20),
        cost_estimate=pl.CostEstimate(
            flops=0, bytes_accessed=4 * array.size, transcendentals=0
        ),
    )(index, array)


def dot(a, b):
    return jnp.dot(a, b, preferred_element_type=F32)


def body(activations, grad_output, projector, first_moment, second_moment):
    place = lax.axis_index("fsdp").astype(jnp.int32)
    tp_place = lax.axis_index("tp").astype(jnp.int32)
    core = place & 1
    chip = place >> 1
    tokens, width = grad_output.shape
    half = width // 2
    quarter = half // 2
    rank = projector.shape[1]
    rank_block = rank // 16
    column_count = rank // 8

    def my_half(array):
        return lax.dynamic_slice_in_dim(array, core * half, half, 1)

    def other_half(array):
        return lax.dynamic_slice_in_dim(array, (1 - core) * half, half, 1)

    block = lax.dynamic_slice_in_dim(projector, tp_place * column_count, column_count, 1)
    split = block.shape[0] // 2
    orders = ([8, 24, 2, 6], [24, 8, 6, 2])
    parts = [gather(block[h * split : (h + 1) * split], "fsdp", orders[h]) for h in range(2)]
    columns = jnp.concatenate(parts, axis=0)
    columns_other = swap(columns, "fsdp", 1)
    index = jnp.concatenate(
        [2 * (place ^ c ^ table(doubled(orders[h]))) + h for c in range(2) for h in range(2)]
    )
    act = reorder(activations, index, split)
    depth = columns.shape[0]
    dims = (((0,), (1,)), ((), ()))
    own = lax.dot_general(columns, act[:, :depth], dims, preferred_element_type=F32)
    own = own + lax.dot_general(columns_other, act[:, depth:], dims, preferred_element_type=F32)
    own = own.astype(BF)

    tp_orders = ([1, 2, 6], [6, 1, 2])
    coords = jnp.concatenate(
        [gather(own[h * rank_block : (h + 1) * rank_block], "tp", tp_orders[h]) for h in range(2)],
        axis=0,
    )
    coords = jnp.concatenate([coords, swap(coords, "fsdp", 1)], axis=1)
    have = expand(
        jnp.concatenate([2 * (tp_place ^ table(doubled(tp_orders[h]))) + h for h in range(2)]),
        rank_block,
    )

    grads = jnp.concatenate(
        [my_half(grad_output), swap(other_half(grad_output), "fsdp", 1)], axis=0
    )
    moments = jnp.concatenate([first_moment, second_moment], axis=0)
    moments_other = swap(other_half(moments), "fsdp", 1)
    moments_own = my_half(moments)
    rows = first_moment.shape[0]
    first = by_core(core, moments_own[:rows], moments_other[:rows], 0)
    second = by_core(core, moments_own[rows:], moments_other[rows:], 0)
    projector_other = swap(projector, "fsdp", 1)

    sums = []
    sum_orders = ([1, 3, 4, 12], [3, 1, 12, 4])
    for h in range(2):
        wanted = expand(chip ^ table(doubled(sum_orders[h][::-1])), rank_block)
        grads_part = grads[:, h * quarter : (h + 1) * quarter]
        keep_rows = rank // 2
        chosen = dot(one_hot(wanted[keep_rows:], have), coords).astype(BF)
        sent = dot(chosen, grads_part).astype(BF)
        chosen = dot(one_hot(wanted[:keep_rows], have), coords).astype(BF)
        kept = dot(chosen, grads_part)
        for mask in sum_orders[h]:
            total = kept + swap(sent, "fsdp", 2 * mask).astype(F32)
            keep_rows = total.shape[0] // 2
            kept = total[:keep_rows]
            sent = total[keep_rows:].astype(BF)
        sums.append(total)
    lowrank = jnp.concatenate(sums, axis=1)

    new_first = 0.9 * first + 0.1 * lowrank
    new_second = 0.99 * second + 0.01 * lowrank * lowrank
    direction = (new_first / first_fix / (jnp.sqrt(new_second / second_fix) + 1e-08)).astype(BF)

    def rows_of(array, which):
        return lax.dynamic_slice_in_dim(array, which * rows, rows, 0)

    states_other = swap(
        jnp.concatenate([rows_of(new_first, 1 - core), rows_of(new_second, 1 - core)], axis=0),
        "fsdp",
        1,
    )
    out_first = by_core(core, rows_of(new_first, core), states_other[:rows], 1)
    out_second = by_core(core, rows_of(new_second, core), states_other[rows:], 1)

    own_parts, got_parts = [], []
    back_orders = ([4, 12, 1, 3], [12, 4, 3, 1])
    ranks = jnp.arange(rank, dtype=jnp.int32)
    for h in range(2):
        order = expand(chip ^ table(doubled(back_orders[h])), rank_block)
        choose = one_hot(ranks, order)
        own_rows = dot(projector, choose).astype(BF)
        other_rows = dot(projector_other, choose).astype(BF)
        part = gather(
            direction[:, h * quarter : (h + 1) * quarter],
            "fsdp",
            [2 * mask for mask in back_orders[h]],
        )
        got_parts.append(swap(dot(other_rows, part).astype(BF), "fsdp", 1))
        own_parts.append(dot(own_rows, part).astype(BF))
    update = by_core(
        core, jnp.concatenate(own_parts, axis=1), jnp.concatenate(got_parts, axis=1), 1
    )
    return (out_first, out_second, update)


def solution(mesh):
    return jax.shard_map(
        body,
        mesh=mesh,
        in_specs=(
            P("fsdp", None),
            P("fsdp", "tp"),
            P("fsdp", None),
            P("fsdp", "tp"),
            P("fsdp", "tp"),
        ),
        out_specs=(P("fsdp", "tp"), P("fsdp", "tp"), P("fsdp", "tp")),
        check_vma=False,
    )
```

```python
import functools

import jax
import jax.numpy as jnp
from jax import lax
from jax.experimental import pallas as pl
from jax.experimental.pallas import tpu as pltpu
from jax.sharding import PartitionSpec as P

first_fix = 0.9999734386011124
second_fix = 0.6339676587267705
BF = jnp.bfloat16
F32 = jnp.float32
MIB = 2**20


def swap(array, axis, mask):
    count = lax.axis_size(axis)
    return lax.ppermute(array, axis, [(i, i ^ mask) for i in range(count)])


def doubled(masks):
    order = [0]
    for mask in masks:
        order = order + [o ^ mask for o in order]
    return order


def table(order):
    return jnp.array(order, dtype=jnp.int32)


def by_core(core, own, other, axis):
    return jnp.where(
        core == 0,
        jnp.concatenate([own, other], axis=axis),
        jnp.concatenate([other, own], axis=axis),
    )


def call(kernel, outs, args, flops=0, vmem=16, scratch=(), smem=0):
    moved = sum(a.size * a.dtype.itemsize for a in args)
    moved += sum(o.size * o.dtype.itemsize for o in outs)
    specs = [
        pl.BlockSpec(memory_space=pltpu.SMEM if i < smem else pltpu.VMEM)
        for i in range(len(args))
    ]
    return pl.pallas_call(
        kernel,
        out_shape=list(outs),
        in_specs=specs,
        out_specs=[pl.BlockSpec(memory_space=pltpu.VMEM) for _ in outs],
        scratch_shapes=list(scratch),
        compiler_params=pltpu.CompilerParams(vmem_limit_bytes=vmem * MIB),
        cost_estimate=pl.CostEstimate(flops=flops, bytes_accessed=moved, transcendentals=0),
    )(*args)


def shape(rows, columns, kind):
    return jax.ShapeDtypeStruct((rows, columns), kind)


def stack_kernel(sizes, *refs):
    outs = refs[sum(sizes) :]
    at = 0
    for size, out_ref in zip(sizes, outs):
        row = 0
        for ref in refs[at : at + size]:
            out_ref[row : row + ref.shape[0], :] = ref[...]
            row += ref.shape[0]
        at += size


def stack(groups):
    outs = [shape(sum(a.shape[0] for a in g), g[0].shape[1], g[0].dtype) for g in groups]
    return call(
        functools.partial(stack_kernel, [len(g) for g in groups]),
        outs,
        [a for g in groups for a in g],
    )


def reorder_kernel(width, index_ref, in_ref, out_ref):
    for k in range(out_ref.shape[1] // width):
        start = pl.multiple_of(index_ref[k] * width, width)
        out_ref[:, k * width : (k + 1) * width] = in_ref[:, pl.ds(start, width)]


def reorder(array, index, width):
    outs = [shape(array.shape[0], array.shape[1], array.dtype)]
    return call(
        functools.partial(reorder_kernel, width), outs, [index, array], vmem=24, smem=1
    )[0]


def sums_kernel(count, block, index_ref, own_ref, other_ref, grads_ref, *refs):
    outs, chosen = refs[:count], refs[count]
    tokens = own_ref.shape[1]
    at = 0
    for part, out_ref in enumerate(outs):
        blocks = out_ref.shape[0] // block
        for k in range(blocks):
            start = pl.multiple_of(index_ref[part * blocks + k] * block, block)
            chosen[k * block : (k + 1) * block, :tokens] = own_ref[pl.ds(start, block), :]
            chosen[k * block : (k + 1) * block, tokens:] = other_ref[pl.ds(start, block), :]
        width = out_ref.shape[1]
        out_ref[...] = jnp.dot(
            chosen[...], grads_ref[:, at : at + width], preferred_element_type=F32
        ).astype(out_ref.dtype)
        at += width


def partial_sums(index, own, other, grads, rows, widths, block, kind):
    return call(
        functools.partial(sums_kernel, len(widths), block),
        [shape(rows, w, kind) for w in widths],
        [index, own, other, grads],
        flops=2 * rows * grads.size,
        vmem=24,
        scratch=[pltpu.VMEM((rows, 2 * own.shape[1]), BF)],
        smem=1,
    )


def halve_kernel(count, *refs):
    kept, got, kept_out, sent = (refs[i * count : (i + 1) * count] for i in range(4))
    for k, g, o, s in zip(kept, got, kept_out, sent):
        rows = o.shape[0]
        s[...] = (k[rows:, :] + g[rows:, :].astype(F32)).astype(s.dtype)
        o[...] = k[:rows, :] + g[:rows, :].astype(F32)


def halve(kept, got):
    rows = kept[0].shape[0] // 2
    outs = [shape(rows, k.shape[1], kind) for kind in (F32, BF) for k in kept]
    result = call(functools.partial(halve_kernel, len(kept)), outs, list(kept) + list(got))
    return result[: len(kept)], result[len(kept) :]


def adam_kernel(count, *refs):
    kept, got = refs[:count], refs[count : 2 * count]
    first_ref, second_ref = refs[2 * count : 2 * count + 2]
    new_first_ref, new_second_ref = refs[2 * count + 2 : 2 * count + 4]
    directions = refs[2 * count + 4 :]
    at = 0
    for k, g, d in zip(kept, got, directions):
        span = slice(at, at + k.shape[1])
        at += k.shape[1]
        lowrank = k[...] + g[...].astype(F32)
        new_first = 0.9 * first_ref[:, span] + 0.1 * lowrank
        new_second = 0.99 * second_ref[:, span] + 0.01 * lowrank * lowrank
        new_first_ref[:, span] = new_first
        new_second_ref[:, span] = new_second
        d[...] = (new_first / first_fix / (jnp.sqrt(new_second / second_fix) + 1e-08)).astype(
            d.dtype
        )


def adam(kept, got, first, second):
    outs = [shape(*first.shape, F32)] * 2 + [shape(*k.shape, BF) for k in kept]
    result = call(
        functools.partial(adam_kernel, len(kept)), outs, [*kept, *got, first, second]
    )
    return result[0], result[1], result[2:]


def early_kernel(count, *refs):
    factors, parts, out_ref = refs[:count], refs[count : 2 * count], refs[2 * count]
    at = 0
    for f, p in zip(factors, parts):
        depth, width = p.shape
        out_ref[:, at : at + width] = jnp.dot(
            f[:, :depth], p[...], preferred_element_type=F32
        )
        at += width


def late_kernel(count, row, *refs):
    factors, parts, sum_ref, out_ref = (
        refs[:count],
        refs[count : 2 * count],
        refs[2 * count],
        refs[2 * count + 1],
    )
    rows = out_ref.shape[0]
    at = 0
    for f, p in zip(factors, parts):
        depth, width = p.shape
        product = jnp.dot(f[row : row + rows, depth:], p[...], preferred_element_type=F32)
        out_ref[:, at : at + width] = (
            sum_ref[row : row + rows, at : at + width] + product
        ).astype(out_ref.dtype)
        at += width


def body(activations, grad_output, projector, first_moment, second_moment):
    place = lax.axis_index("fsdp").astype(jnp.int32)
    tp_place = lax.axis_index("tp").astype(jnp.int32)
    core = place & 1
    chip = place >> 1
    tokens, width = grad_output.shape
    half = width // 2
    rank = projector.shape[1]
    block = rank // 16
    column_count = rank // 8
    wide = half * 5 // 14
    widths = (wide, wide, half // 2 - wide, half // 2 - wide)
    rows = first_moment.shape[0]

    def my_half(array):
        return lax.dynamic_slice_in_dim(array, core * half, half, 1)

    def other_half(array):
        return lax.dynamic_slice_in_dim(array, (1 - core) * half, half, 1)

    columns = lax.dynamic_slice_in_dim(projector, tp_place * column_count, column_count, 1)
    columns = stack([[columns] + [swap(columns, "fsdp", m) for m in (8, 16, 24)]])[0]
    columns = stack([[columns] + [swap(columns, "fsdp", m) for m in (2, 4, 6)]])[0]
    columns_other = swap(columns, "fsdp", 1)
    order = [x + z for x in (0, 2, 4, 6) for z in (0, 8, 16, 24)]
    index = jnp.concatenate([place ^ c ^ table(order) for c in range(2)])
    act = reorder(activations, index, projector.shape[0])
    depth = columns.shape[0]
    dims = (((0,), (1,)), ((), ()))
    own = lax.dot_general(columns, act[:, :depth], dims, preferred_element_type=F32)
    own = own + lax.dot_general(columns_other, act[:, depth:], dims, preferred_element_type=F32)
    own = own.astype(BF)

    coords = stack([[own, swap(own, "tp", 1)]])[0]
    coords = stack([[coords] + [swap(coords, "tp", m) for m in (2, 4, 6)]])[0]
    coords_other = swap(coords, "fsdp", 1)

    grads = jnp.concatenate(
        [my_half(grad_output), swap(other_half(grad_output), "fsdp", 1)], axis=0
    )
    moments = jnp.concatenate([first_moment, second_moment], axis=0)
    moments_other = swap(other_half(moments), "fsdp", 1)
    moments_own = my_half(moments)
    first = by_core(core, moments_own[:rows], moments_other[:rows], 0)
    second = by_core(core, moments_own[rows:], moments_other[rows:], 0)
    both = jnp.concatenate([projector, swap(projector, "fsdp", 1)], axis=0)

    sum_orders = ([1, 3, 4, 12], [3, 1, 12, 4], [4, 12, 1, 3], [12, 4, 3, 1])
    keep_index, send_index = [], []
    for masks in sum_orders:
        wanted = chip ^ table(doubled(masks[::-1]))
        position = 2 * (tp_place ^ (wanted >> 1)) + (wanted & 1)
        keep_index.append(position[:8])
        send_index.append(position[8:])
    arrays = (coords, coords_other, grads, rank // 2, widths, block)
    sent = partial_sums(jnp.concatenate(send_index), *arrays, BF)
    kept = partial_sums(jnp.concatenate(keep_index), *arrays, F32)
    for stage in range(3):
        got = [swap(s, "fsdp", 2 * m[stage]) for s, m in zip(sent, sum_orders)]
        kept, sent = halve(kept, got)
    got = [swap(s, "fsdp", 2 * m[3]) for s, m in zip(sent, sum_orders)]
    new_first, new_second, parts = adam(kept, got, first, second)

    def rows_of(array, which):
        return lax.dynamic_slice_in_dim(array, which * rows, rows, 0)

    states_other = swap(
        jnp.concatenate([rows_of(new_first, 1 - core), rows_of(new_second, 1 - core)], axis=0),
        "fsdp",
        1,
    )
    out_first = by_core(core, rows_of(new_first, core), states_other[:rows], 1)
    out_second = by_core(core, rows_of(new_second, core), states_other[rows:], 1)

    back_orders = [m[::-1] for m in sum_orders]
    ranks = jnp.arange(rank, dtype=jnp.int32)
    factors = []
    for masks in back_orders:
        blocks = chip ^ table(doubled(masks))
        wanted = (blocks[:, None] * block + ranks[None, :block]).reshape(-1)
        choose = (ranks[:, None] == wanted[None, :]).astype(BF)
        factors.append(jnp.dot(both, choose, preferred_element_type=F32).astype(BF))
    for stage in range(4):
        got = [swap(p, "fsdp", 2 * m[stage]) for p, m in zip(parts, back_orders)]
        if stage < 3:
            parts = stack([[p, g] for p, g in zip(parts, got)])
    count = len(parts)
    flops = rank * half * both.shape[0]
    early = call(
        functools.partial(early_kernel, count),
        [shape(both.shape[0], half, F32)],
        [*factors, *parts],
        flops=flops,
        vmem=32,
    )[0]
    late = [
        call(
            functools.partial(late_kernel, count, row),
            [shape(tokens, half, BF)],
            [*factors, *got, early],
            flops=flops // 2,
            vmem=32,
        )[0]
        for row in (tokens, 0)
    ]
    update = by_core(core, late[1], swap(late[0], "fsdp", 1), 1)
    return (out_first, out_second, update)


def solution(mesh):
    return jax.shard_map(
        body,
        mesh=mesh,
        in_specs=(
            P("fsdp", None),
            P("fsdp", "tp"),
            P("fsdp", None),
            P("fsdp", "tp"),
            P("fsdp", "tp"),
        ),
        out_specs=(P("fsdp", "tp"), P("fsdp", "tp"), P("fsdp", "tp")),
        check_vma=False,
    )
```

```python
import functools

import jax
import jax.numpy as jnp
from jax import lax
from jax.experimental import pallas as pl
from jax.experimental.pallas import tpu as pltpu
from jax.sharding import PartitionSpec as P

first_fix = 0.9999734386011124
second_fix = 0.6339676587267705
BF = jnp.bfloat16
F32 = jnp.float32
MIB = 2**20


def swap(array, axis, mask):
    count = lax.axis_size(axis)
    return lax.ppermute(array, axis, [(i, i ^ mask) for i in range(count)])


def doubled(masks):
    order = [0]
    for mask in masks:
        order = order + [o ^ mask for o in order]
    return order


def table(order):
    return jnp.array(order, dtype=jnp.int32)


def by_core(core, own, other, axis):
    return jnp.where(
        core == 0,
        jnp.concatenate([own, other], axis=axis),
        jnp.concatenate([other, own], axis=axis),
    )


class Chain:
    def __init__(self):
        self.token = jnp.zeros((8, 128), jnp.int32)

    def __call__(self, kernel, outs, args, **options):
        token = shape(8, 128, jnp.int32)
        inputs, results = len(args), len(outs)

        def chained(*refs):
            refs[inputs + 1 + results][...] = refs[inputs][...]
            kernel(
                *refs[:inputs],
                *refs[inputs + 1 : inputs + 1 + results],
                *refs[inputs + 2 + results :],
            )

        *result, self.token = call(chained, [*outs, token], [*args, self.token], **options)
        return result


def call(kernel, outs, args, flops=0, vmem=16, scratch=(), smem=0):
    moved = sum(a.size * a.dtype.itemsize for a in args)
    moved += sum(o.size * o.dtype.itemsize for o in outs)
    specs = [
        pl.BlockSpec(memory_space=pltpu.SMEM if i < smem else pltpu.VMEM)
        for i in range(len(args))
    ]
    return pl.pallas_call(
        kernel,
        out_shape=list(outs),
        in_specs=specs,
        out_specs=[pl.BlockSpec(memory_space=pltpu.VMEM) for _ in outs],
        scratch_shapes=list(scratch),
        compiler_params=pltpu.CompilerParams(vmem_limit_bytes=vmem * MIB),
        cost_estimate=pl.CostEstimate(flops=flops, bytes_accessed=moved, transcendentals=0),
    )(*args)


def shape(rows, columns, kind):
    return jax.ShapeDtypeStruct((rows, columns), kind)


def stack_kernel(sizes, *refs):
    outs = refs[sum(sizes) :]
    at = 0
    for size, out_ref in zip(sizes, outs):
        row = 0
        for ref in refs[at : at + size]:
            out_ref[row : row + ref.shape[0], :] = ref[...]
            row += ref.shape[0]
        at += size


def stack(groups, run=call):
    outs = [shape(sum(a.shape[0] for a in g), g[0].shape[1], g[0].dtype) for g in groups]
    return run(
        functools.partial(stack_kernel, [len(g) for g in groups]),
        outs,
        [a for g in groups for a in g],
    )


def reorder_kernel(width, index_ref, in_ref, out_ref):
    for k in range(out_ref.shape[1] // width):
        start = pl.multiple_of(index_ref[k] * width, width)
        out_ref[:, k * width : (k + 1) * width] = in_ref[:, pl.ds(start, width)]


def reorder(array, index, width):
    outs = [shape(array.shape[0], array.shape[1], array.dtype)]
    return call(
        functools.partial(reorder_kernel, width), outs, [index, array], vmem=24, smem=1
    )[0]


def sums_kernel(count, block, at, index_ref, own_ref, other_ref, grads_ref, *refs):
    outs, chosen = refs[:count], refs[count]
    tokens = own_ref.shape[1]
    for part, out_ref in enumerate(outs):
        blocks = out_ref.shape[0] // block
        for k in range(blocks):
            start = pl.multiple_of(index_ref[part * blocks + k] * block, block)
            chosen[k * block : (k + 1) * block, :tokens] = own_ref[pl.ds(start, block), :]
            chosen[k * block : (k + 1) * block, tokens:] = other_ref[pl.ds(start, block), :]
        width = out_ref.shape[1]
        out_ref[...] = jnp.dot(
            chosen[...], grads_ref[:, at : at + width], preferred_element_type=F32
        ).astype(out_ref.dtype)
        at += width


def partial_sums(run, index, own, other, grads, rows, at, widths, block, kind):
    return run(
        functools.partial(sums_kernel, len(widths), block, at),
        [shape(rows, w, kind) for w in widths],
        [index, own, other, grads],
        flops=4 * rows * own.shape[1] * sum(widths),
        vmem=24,
        scratch=[pltpu.VMEM((rows, 2 * own.shape[1]), BF)],
        smem=1,
    )


def halve_kernel(count, *refs):
    kept, got, kept_out, sent = (refs[i * count : (i + 1) * count] for i in range(4))
    for k, g, o, s in zip(kept, got, kept_out, sent):
        rows = o.shape[0]
        s[...] = (k[rows:, :] + g[rows:, :].astype(F32)).astype(s.dtype)
        o[...] = k[:rows, :] + g[:rows, :].astype(F32)


def halve(run, kept, got):
    rows = kept[0].shape[0] // 2
    outs = [shape(rows, k.shape[1], kind) for kind in (F32, BF) for k in kept]
    result = run(functools.partial(halve_kernel, len(kept)), outs, list(kept) + list(got))
    return result[: len(kept)], result[len(kept) :]


def adam_kernel(count, at, *refs):
    kept, got = refs[:count], refs[count : 2 * count]
    first_ref, second_ref = refs[2 * count : 2 * count + 2]
    new_first_ref, new_second_ref = refs[2 * count + 2 : 2 * count + 4]
    directions = refs[2 * count + 4 :]
    to = 0
    for k, g, d in zip(kept, got, directions):
        width = k.shape[1]
        lowrank = k[...] + g[...].astype(F32)
        new_first = 0.9 * first_ref[:, at : at + width] + 0.1 * lowrank
        new_second = 0.99 * second_ref[:, at : at + width] + 0.01 * lowrank * lowrank
        new_first_ref[:, to : to + width] = new_first
        new_second_ref[:, to : to + width] = new_second
        d[...] = (new_first / first_fix / (jnp.sqrt(new_second / second_fix) + 1e-08)).astype(
            d.dtype
        )
        at += width
        to += width


def adam(run, kept, got, first, second, at):
    rows, width = kept[0].shape[0], sum(k.shape[1] for k in kept)
    outs = [shape(rows, width, F32)] * 2 + [shape(*k.shape, BF) for k in kept]
    result = run(
        functools.partial(adam_kernel, len(kept), at), outs, [*kept, *got, first, second]
    )
    return result[0], result[1], result[2:]


def early_kernel(count, *refs):
    factors, parts, out_ref = refs[:count], refs[count : 2 * count], refs[2 * count]
    at = 0
    for f, p in zip(factors, parts):
        depth, width = p.shape
        out_ref[:, at : at + width] = jnp.dot(
            f[:, :depth], p[...], preferred_element_type=F32
        )
        at += width


def late_kernel(count, row, *refs):
    factors, parts, sum_ref, out_ref = (
        refs[:count],
        refs[count : 2 * count],
        refs[2 * count],
        refs[2 * count + 1],
    )
    rows = out_ref.shape[0]
    at = 0
    for f, p in zip(factors, parts):
        depth, width = p.shape
        product = jnp.dot(f[row : row + rows, depth:], p[...], preferred_element_type=F32)
        out_ref[:, at : at + width] = (
            sum_ref[row : row + rows, at : at + width] + product
        ).astype(out_ref.dtype)
        at += width


def body(activations, grad_output, projector, first_moment, second_moment):
    place = lax.axis_index("fsdp").astype(jnp.int32)
    tp_place = lax.axis_index("tp").astype(jnp.int32)
    core = place & 1
    chip = place >> 1
    tokens, width = grad_output.shape
    half = width // 2
    rank = projector.shape[1]
    block = rank // 16
    column_count = rank // 8
    wide = half * 2 // 7
    narrow = half // 2 - wide
    waves = ((wide, narrow), (narrow, wide))
    offsets = (0, half // 2)
    rows = first_moment.shape[0]

    def my_half(array):
        return lax.dynamic_slice_in_dim(array, core * half, half, 1)

    def other_half(array):
        return lax.dynamic_slice_in_dim(array, (1 - core) * half, half, 1)

    columns = lax.dynamic_slice_in_dim(projector, tp_place * column_count, column_count, 1)
    columns = stack([[columns] + [swap(columns, "fsdp", m) for m in (8, 16, 24)]])[0]
    columns = stack([[columns] + [swap(columns, "fsdp", m) for m in (2, 4, 6)]])[0]
    columns_other = swap(columns, "fsdp", 1)
    order = [x + z for x in (0, 2, 4, 6) for z in (0, 8, 16, 24)]
    index = jnp.concatenate([place ^ c ^ table(order) for c in range(2)])
    act = reorder(activations, index, projector.shape[0])
    depth = columns.shape[0]
    dims = (((0,), (1,)), ((), ()))
    own = lax.dot_general(columns, act[:, :depth], dims, preferred_element_type=F32)
    own = own + lax.dot_general(columns_other, act[:, depth:], dims, preferred_element_type=F32)
    own = own.astype(BF)

    coords = stack([[own, swap(own, "tp", 1)]])[0]
    coords = stack([[coords] + [swap(coords, "tp", m) for m in (2, 4, 6)]])[0]
    coords_other = swap(coords, "fsdp", 1)

    grads = jnp.concatenate(
        [my_half(grad_output), swap(other_half(grad_output), "fsdp", 1)], axis=0
    )
    moments = jnp.concatenate([first_moment, second_moment], axis=0)
    moments_other = swap(other_half(moments), "fsdp", 1)
    moments_own = my_half(moments)
    first = by_core(core, moments_own[:rows], moments_other[:rows], 0)
    second = by_core(core, moments_own[rows:], moments_other[rows:], 0)
    both = jnp.concatenate([projector, swap(projector, "fsdp", 1)], axis=0)

    sum_orders = ([1, 3, 4, 12], [3, 1, 12, 4])
    back_orders = [m[::-1] for m in sum_orders]
    keep_index, send_index = [], []
    for masks in sum_orders:
        wanted = chip ^ table(doubled(masks[::-1]))
        position = 2 * (tp_place ^ (wanted >> 1)) + (wanted & 1)
        keep_index.append(position[:8])
        send_index.append(position[8:])
    keep_index, send_index = jnp.concatenate(keep_index), jnp.concatenate(send_index)
    ranks = jnp.arange(rank, dtype=jnp.int32)
    factors = []
    for masks in back_orders:
        blocks = chip ^ table(doubled(masks))
        wanted = (blocks[:, None] * block + ranks[None, :block]).reshape(-1)
        choose = (ranks[:, None] == wanted[None, :]).astype(BF)
        factors.append(jnp.dot(both, choose, preferred_element_type=F32).astype(BF))

    run = Chain()
    sent, kept, parts, got, states = {}, {}, {}, {}, {}

    def sums(w, index, kind):
        return partial_sums(
            run, index, coords, coords_other, grads, rank // 2, offsets[w], waves[w], block, kind
        )

    def exchange(w, stage):
        if stage < 4:
            pairs = zip(sent[w], [m[stage] for m in sum_orders])
        else:
            pairs = zip(parts[w], [m[stage - 4] for m in back_orders])
        got[w] = [swap(array, "fsdp", 2 * mask) for array, mask in pairs]

    def advance(w, stage):
        if stage < 3:
            kept[w], sent[w] = halve(run, kept[w], got[w])
        elif stage == 3:
            new_first, new_second, parts[w] = adam(
                run, kept[w], got[w], first, second, offsets[w]
            )
            states[w] = (new_first, new_second)
        else:
            parts[w] = stack([[p, g] for p, g in zip(parts[w], got[w])], run)
        exchange(w, stage + 1)

    def early(w):
        return run(
            functools.partial(early_kernel, 2),
            [shape(2 * tokens, half // 2, F32)],
            [*factors, *parts[w]],
            flops=rank * half * tokens,
            vmem=24,
        )[0]

    def late(w, summed, row):
        return run(
            functools.partial(late_kernel, 2, row),
            [shape(tokens, half // 2, BF)],
            [*factors, *got[w], summed],
            flops=rank * half * tokens // 2,
            vmem=24,
        )[0]

    sent[0] = sums(0, send_index, BF)
    exchange(0, 0)
    kept[0] = sums(0, keep_index, F32)
    kept[1] = sums(1, keep_index, F32)
    advance(0, 0)
    sent[1] = sums(1, send_index, BF)
    exchange(1, 0)
    advance(0, 1)
    for stage in range(5):
        advance(1, stage)
        advance(0, stage + 2)
    summed = early(0)
    advance(1, 5)
    other = [swap(late(0, summed, tokens), "fsdp", 1)]
    own = [late(0, summed, 0)]
    advance(1, 6)
    summed = early(1)
    other.append(swap(late(1, summed, tokens), "fsdp", 1))
    own.append(late(1, summed, 0))
    update = by_core(core, jnp.concatenate(own, axis=1), jnp.concatenate(other, axis=1), 1)

    def rows_of(array, which):
        return lax.dynamic_slice_in_dim(array, which * rows, rows, 0)

    new_first, new_second = (
        jnp.concatenate([states[0][k], states[1][k]], axis=1) for k in range(2)
    )
    states_other = swap(
        jnp.concatenate([rows_of(new_first, 1 - core), rows_of(new_second, 1 - core)], axis=0),
        "fsdp",
        1,
    )
    out_first = by_core(core, rows_of(new_first, core), states_other[:rows], 1)
    out_second = by_core(core, rows_of(new_second, core), states_other[rows:], 1)
    return (out_first, out_second, update)


def solution(mesh):
    return jax.shard_map(
        body,
        mesh=mesh,
        in_specs=(
            P("fsdp", None),
            P("fsdp", "tp"),
            P("fsdp", None),
            P("fsdp", "tp"),
            P("fsdp", "tp"),
        ),
        out_specs=(P("fsdp", "tp"), P("fsdp", "tp"), P("fsdp", "tp")),
        check_vma=False,
    )
```

```python
import functools

import jax
import jax.numpy as jnp
from jax import lax
from jax.experimental import pallas as pl
from jax.experimental.pallas import tpu as pltpu
from jax.sharding import PartitionSpec as P

first_fix = 0.9999734386011124
second_fix = 0.6339676587267705
BF = jnp.bfloat16
F32 = jnp.float32
MIB = 2**20


def swap(array, axis, mask):
    count = lax.axis_size(axis)
    return lax.ppermute(array, axis, [(i, i ^ mask) for i in range(count)])


def doubled(masks):
    order = [0]
    for mask in masks:
        order = order + [o ^ mask for o in order]
    return order


def table(order):
    return jnp.array(order, dtype=jnp.int32)


def by_core(core, own, other, axis):
    return jnp.where(
        core == 0,
        jnp.concatenate([own, other], axis=axis),
        jnp.concatenate([other, own], axis=axis),
    )


def call(kernel, outs, args, flops=0, vmem=16, scratch=(), smem=0, after=()):
    moved = sum(a.size * a.dtype.itemsize for a in args)
    moved += sum(o.size * o.dtype.itemsize for o in outs)
    specs = [
        pl.BlockSpec(memory_space=pltpu.SMEM if i < smem else pltpu.VMEM)
        for i in range(len(args))
    ]
    count = len(args)

    def body(*refs):
        kernel(*refs[:count], *refs[count + len(after) :])

    specs += [pl.BlockSpec(memory_space=pl.ANY) for _ in after]
    return pl.pallas_call(
        body,
        out_shape=list(outs),
        in_specs=specs,
        out_specs=[pl.BlockSpec(memory_space=pltpu.VMEM) for _ in outs],
        scratch_shapes=list(scratch),
        compiler_params=pltpu.CompilerParams(vmem_limit_bytes=vmem * MIB),
        cost_estimate=pl.CostEstimate(flops=flops, bytes_accessed=moved, transcendentals=0),
    )(*args, *after)


def shape(rows, columns, kind):
    return jax.ShapeDtypeStruct((rows, columns), kind)


def stack_kernel(sizes, *refs):
    outs = refs[sum(sizes) :]
    at = 0
    for size, out_ref in zip(sizes, outs):
        row = 0
        for ref in refs[at : at + size]:
            out_ref[row : row + ref.shape[0], :] = ref[...]
            row += ref.shape[0]
        at += size


def stack(groups):
    outs = [shape(sum(a.shape[0] for a in g), g[0].shape[1], g[0].dtype) for g in groups]
    return call(
        functools.partial(stack_kernel, [len(g) for g in groups]),
        outs,
        [a for g in groups for a in g],
    )


def reorder_kernel(width, index_ref, in_ref, out_ref):
    for k in range(out_ref.shape[1] // width):
        start = pl.multiple_of(index_ref[k] * width, width)
        out_ref[:, k * width : (k + 1) * width] = in_ref[:, pl.ds(start, width)]


def reorder(array, index, width):
    outs = [shape(array.shape[0], array.shape[1], array.dtype)]
    return call(
        functools.partial(reorder_kernel, width), outs, [index, array], vmem=24, smem=1
    )[0]


def sums_kernel(count, block, index_ref, own_ref, other_ref, grads_ref, *refs):
    outs, chosen = refs[:count], refs[count]
    tokens = own_ref.shape[1]
    at = 0
    for part, out_ref in enumerate(outs):
        blocks = out_ref.shape[0] // block
        for k in range(blocks):
            start = pl.multiple_of(index_ref[part * blocks + k] * block, block)
            chosen[k * block : (k + 1) * block, :tokens] = own_ref[pl.ds(start, block), :]
            chosen[k * block : (k + 1) * block, tokens:] = other_ref[pl.ds(start, block), :]
        width = out_ref.shape[1]
        out_ref[...] = jnp.dot(
            chosen[...], grads_ref[:, at : at + width], preferred_element_type=F32
        ).astype(out_ref.dtype)
        at += width


def partial_sums(index, own, other, grads, rows, widths, block, kind, after=()):
    return call(
        functools.partial(sums_kernel, len(widths), block),
        [shape(rows, w, kind) for w in widths],
        [index, own, other, grads],
        flops=2 * rows * grads.size,
        vmem=24,
        scratch=[pltpu.VMEM((rows, 2 * own.shape[1]), BF)],
        smem=1,
        after=after,
    )


def halve_kernel(count, *refs):
    kept, got, kept_out, sent = (refs[i * count : (i + 1) * count] for i in range(4))
    for k, g, o, s in zip(kept, got, kept_out, sent):
        rows = o.shape[0]
        s[...] = (k[rows:, :] + g[rows:, :].astype(F32)).astype(s.dtype)
        o[...] = k[:rows, :] + g[:rows, :].astype(F32)


def halve(kept, got):
    rows = kept[0].shape[0] // 2
    outs = [shape(rows, k.shape[1], kind) for kind in (F32, BF) for k in kept]
    result = call(functools.partial(halve_kernel, len(kept)), outs, list(kept) + list(got))
    return result[: len(kept)], result[len(kept) :]


def adam_kernel(count, *refs):
    kept, got = refs[:count], refs[count : 2 * count]
    first_ref, second_ref = refs[2 * count : 2 * count + 2]
    new_first_ref, new_second_ref = refs[2 * count + 2 : 2 * count + 4]
    directions = refs[2 * count + 4 :]
    at = 0
    for k, g, d in zip(kept, got, directions):
        span = slice(at, at + k.shape[1])
        at += k.shape[1]
        lowrank = k[...] + g[...].astype(F32)
        new_first = 0.9 * first_ref[:, span] + 0.1 * lowrank
        new_second = 0.99 * second_ref[:, span] + 0.01 * lowrank * lowrank
        new_first_ref[:, span] = new_first
        new_second_ref[:, span] = new_second
        d[...] = (new_first / first_fix / (jnp.sqrt(new_second / second_fix) + 1e-08)).astype(
            d.dtype
        )


def adam(kept, got, first, second):
    outs = [shape(*first.shape, F32)] * 2 + [shape(*k.shape, BF) for k in kept]
    result = call(
        functools.partial(adam_kernel, len(kept)), outs, [*kept, *got, first, second]
    )
    return result[0], result[1], result[2:]


def early_kernel(count, *refs):
    factors, parts, out_ref = refs[:count], refs[count : 2 * count], refs[2 * count]
    at = 0
    for f, p in zip(factors, parts):
        depth, width = p.shape
        out_ref[:, at : at + width] = jnp.dot(
            f[:, :depth], p[...], preferred_element_type=F32
        )
        at += width


def late_kernel(count, row, *refs):
    factors, parts, sum_ref, out_ref = (
        refs[:count],
        refs[count : 2 * count],
        refs[2 * count],
        refs[2 * count + 1],
    )
    rows = out_ref.shape[0]
    at = 0
    for f, p in zip(factors, parts):
        depth, width = p.shape
        product = jnp.dot(f[row : row + rows, depth:], p[...], preferred_element_type=F32)
        out_ref[:, at : at + width] = (
            sum_ref[row : row + rows, at : at + width] + product
        ).astype(out_ref.dtype)
        at += width


def body(activations, grad_output, projector, first_moment, second_moment):
    place = lax.axis_index("fsdp").astype(jnp.int32)
    tp_place = lax.axis_index("tp").astype(jnp.int32)
    core = place & 1
    chip = place >> 1
    tokens, width = grad_output.shape
    half = width // 2
    rank = projector.shape[1]
    block = rank // 16
    column_count = rank // 8
    wide = half * 3 // 7
    widths = (wide, wide, half - 2 * wide)
    rows = first_moment.shape[0]

    def my_half(array):
        return lax.dynamic_slice_in_dim(array, core * half, half, 1)

    def other_half(array):
        return lax.dynamic_slice_in_dim(array, (1 - core) * half, half, 1)

    columns = lax.dynamic_slice_in_dim(projector, tp_place * column_count, column_count, 1)
    columns = stack([[columns] + [swap(columns, "fsdp", m) for m in (8, 16, 24)]])[0]
    columns = stack([[columns] + [swap(columns, "fsdp", m) for m in (2, 4, 6)]])[0]
    columns_other = swap(columns, "fsdp", 1)
    order = [x + z for x in (0, 2, 4, 6) for z in (0, 8, 16, 24)]
    index = jnp.concatenate([place ^ c ^ table(order) for c in range(2)])
    act = reorder(activations, index, projector.shape[0])
    depth = columns.shape[0]
    dims = (((0,), (1,)), ((), ()))
    own = lax.dot_general(columns, act[:, :depth], dims, preferred_element_type=F32)
    own = own + lax.dot_general(columns_other, act[:, depth:], dims, preferred_element_type=F32)
    own = own.astype(BF)

    coords = stack([[own, swap(own, "tp", 1)]])[0]
    coords = stack([[coords] + [swap(coords, "tp", m) for m in (2, 4, 6)]])[0]
    coords_other = swap(coords, "fsdp", 1)

    grads = jnp.concatenate(
        [my_half(grad_output), swap(other_half(grad_output), "fsdp", 1)], axis=0
    )
    moments = jnp.concatenate([first_moment, second_moment], axis=0)
    moments_other = swap(other_half(moments), "fsdp", 1)
    moments_own = my_half(moments)
    first = by_core(core, moments_own[:rows], moments_other[:rows], 0)
    second = by_core(core, moments_own[rows:], moments_other[rows:], 0)
    both = jnp.concatenate([projector, swap(projector, "fsdp", 1)], axis=0)

    sum_orders = ([1, 3, 4, 12], [3, 1, 12, 4], [4, 12, 1, 3])
    keep_index, send_index = [], []
    for masks in sum_orders:
        wanted = chip ^ table(doubled(masks[::-1]))
        position = 2 * (tp_place ^ (wanted >> 1)) + (wanted & 1)
        keep_index.append(position[:8])
        send_index.append(position[8:])
    back_orders = [m[::-1] for m in sum_orders]
    ranks = jnp.arange(rank, dtype=jnp.int32)
    factors = []
    for masks in back_orders:
        blocks = chip ^ table(doubled(masks))
        wanted = (blocks[:, None] * block + ranks[None, :block]).reshape(-1)
        choose = (ranks[:, None] == wanted[None, :]).astype(BF)
        factors.append(jnp.dot(both, choose, preferred_element_type=F32).astype(BF))
    arrays = (coords, coords_other, grads, rank // 2, widths, block)
    sent = partial_sums(jnp.concatenate(send_index), *arrays, BF)
    kept = partial_sums(jnp.concatenate(keep_index), *arrays, F32, after=factors)
    for stage in range(3):
        got = [swap(s, "fsdp", 2 * m[stage]) for s, m in zip(sent, sum_orders)]
        kept, sent = halve(kept, got)
    got = [swap(s, "fsdp", 2 * m[3]) for s, m in zip(sent, sum_orders)]
    new_first, new_second, parts = adam(kept, got, first, second)

    def rows_of(array, which):
        return lax.dynamic_slice_in_dim(array, which * rows, rows, 0)

    states_other = swap(
        jnp.concatenate([rows_of(new_first, 1 - core), rows_of(new_second, 1 - core)], axis=0),
        "fsdp",
        1,
    )
    out_first = by_core(core, rows_of(new_first, core), states_other[:rows], 1)
    out_second = by_core(core, rows_of(new_second, core), states_other[rows:], 1)

    for stage in range(4):
        got = [swap(p, "fsdp", 2 * m[stage]) for p, m in zip(parts, back_orders)]
        if stage < 3:
            parts = stack([[p, g] for p, g in zip(parts, got)])
    count = len(parts)
    flops = rank * half * both.shape[0]
    early = call(
        functools.partial(early_kernel, count),
        [shape(both.shape[0], half, F32)],
        [*factors, *parts],
        flops=flops,
        vmem=32,
    )[0]
    late = [
        call(
            functools.partial(late_kernel, count, row),
            [shape(tokens, half, BF)],
            [*factors, *got, early],
            flops=flops // 2,
            vmem=32,
        )[0]
        for row in (tokens, 0)
    ]
    update = by_core(core, late[1], swap(late[0], "fsdp", 1), 1)
    return (out_first, out_second, update)


def solution(mesh):
    return jax.shard_map(
        body,
        mesh=mesh,
        in_specs=(
            P("fsdp", None),
            P("fsdp", "tp"),
            P("fsdp", None),
            P("fsdp", "tp"),
            P("fsdp", "tp"),
        ),
        out_specs=(P("fsdp", "tp"), P("fsdp", "tp"), P("fsdp", "tp")),
        check_vma=False,
    )
```

```python
import functools

import jax
import jax.numpy as jnp
from jax import lax
from jax.experimental import pallas as pl
from jax.experimental.pallas import tpu as pltpu
from jax.sharding import PartitionSpec as P

first_fix = 0.9999734386011124
second_fix = 0.6339676587267705
BF = jnp.bfloat16
F32 = jnp.float32
MIB = 2**20


def swap(array, axis, masks):
    inner = lax.axis_size("tp")
    count = lax.axis_size("fsdp") * inner
    scale = inner if axis == "fsdp" else 1
    return lax.ppermute(
        array, ("fsdp", "tp"), [(i, i ^ (scale * masks[i // inner % 2])) for i in range(count)]
    )


def swap_core(array):
    return swap(array, "fsdp", (1, 1))


def doubled(masks):
    order = [0]
    for mask in masks:
        order = order + [o ^ mask for o in order]
    return order


def table(core, orders):
    first, second = (jnp.array(order, dtype=jnp.int32) for order in orders)
    return jnp.where(core == 0, first, second)


def by_core(core, own, other, axis):
    return jnp.where(
        core == 0,
        jnp.concatenate([own, other], axis=axis),
        jnp.concatenate([other, own], axis=axis),
    )


def call(kernel, outs, args, flops=0, vmem=8, scratch=(), smem=0, after=()):
    moved = sum(a.size * a.dtype.itemsize for a in args)
    moved += sum(o.size * o.dtype.itemsize for o in outs)
    specs = [
        pl.BlockSpec(memory_space=pltpu.SMEM if i < smem else pltpu.VMEM)
        for i in range(len(args))
    ]
    count = len(args)

    def body(*refs):
        kernel(*refs[:count], *refs[count + len(after) :])

    specs += [pl.BlockSpec(memory_space=pl.ANY) for _ in after]
    return pl.pallas_call(
        body,
        out_shape=list(outs),
        in_specs=specs,
        out_specs=[pl.BlockSpec(memory_space=pltpu.VMEM) for _ in outs],
        scratch_shapes=list(scratch),
        compiler_params=pltpu.CompilerParams(vmem_limit_bytes=vmem * MIB),
        cost_estimate=pl.CostEstimate(flops=flops, bytes_accessed=moved, transcendentals=0),
    )(*args, *after)


def shape(rows, columns, kind):
    return jax.ShapeDtypeStruct((rows, columns), kind)


def stack_kernel(sizes, *refs):
    outs = refs[sum(sizes) :]
    at = 0
    for size, out_ref in zip(sizes, outs):
        row = 0
        for ref in refs[at : at + size]:
            out_ref[row : row + ref.shape[0], :] = ref[...]
            row += ref.shape[0]
        at += size


def stack(groups):
    outs = [shape(sum(a.shape[0] for a in g), g[0].shape[1], g[0].dtype) for g in groups]
    return call(
        functools.partial(stack_kernel, [len(g) for g in groups]),
        outs,
        [a for g in groups for a in g],
    )


def reorder_kernel(width, index_ref, in_ref, out_ref):
    for k in range(out_ref.shape[1] // width):
        start = pl.multiple_of(index_ref[k] * width, width)
        out_ref[:, k * width : (k + 1) * width] = in_ref[:, pl.ds(start, width)]


def reorder(array, index, width):
    outs = [shape(array.shape[0], array.shape[1], array.dtype)]
    return call(
        functools.partial(reorder_kernel, width), outs, [index, array], vmem=8, smem=1
    )[0]


def sums_kernel(count, block, index_ref, own_ref, other_ref, grads_ref, *refs):
    outs, chosen = refs[:count], refs[count]
    tokens = own_ref.shape[1]
    at = 0
    for part, out_ref in enumerate(outs):
        blocks = out_ref.shape[0] // block
        for k in range(blocks):
            row = slice(k * block, (k + 1) * block)
            start = pl.multiple_of(index_ref[0, part * blocks + k] * block, block)
            chosen[row, :tokens] = own_ref[pl.ds(start, block), :]
            start = pl.multiple_of(index_ref[1, part * blocks + k] * block, block)
            chosen[row, tokens:] = other_ref[pl.ds(start, block), :]
        width = out_ref.shape[1]
        out_ref[...] = jnp.dot(
            chosen[...], grads_ref[:, at : at + width], preferred_element_type=F32
        ).astype(out_ref.dtype)
        at += width


def partial_sums(index, own, other, grads, rows, widths, block, kind, after=()):
    return call(
        functools.partial(sums_kernel, len(widths), block),
        [shape(rows, w, kind) for w in widths],
        [index, own, other, grads],
        flops=2 * rows * grads.size,
        vmem=12,
        scratch=[pltpu.VMEM((rows, 2 * own.shape[1]), BF)],
        smem=1,
        after=after,
    )


def halve_kernel(count, *refs):
    kept, got, kept_out, sent = (refs[i * count : (i + 1) * count] for i in range(4))
    for k, g, o, s in zip(kept, got, kept_out, sent):
        rows = o.shape[0]
        s[...] = (k[rows:, :] + g[rows:, :].astype(F32)).astype(s.dtype)
        o[...] = k[:rows, :] + g[:rows, :].astype(F32)


def halve(kept, got):
    rows = kept[0].shape[0] // 2
    outs = [shape(rows, k.shape[1], kind) for kind in (F32, BF) for k in kept]
    result = call(functools.partial(halve_kernel, len(kept)), outs, list(kept) + list(got))
    return result[: len(kept)], result[len(kept) :]


def adam_kernel(count, *refs):
    kept, got = refs[:count], refs[count : 2 * count]
    first_ref, second_ref = refs[2 * count : 2 * count + 2]
    new_first_ref, new_second_ref = refs[2 * count + 2 : 2 * count + 4]
    directions = refs[2 * count + 4 :]
    at = 0
    for k, g, d in zip(kept, got, directions):
        span = slice(at, at + k.shape[1])
        at += k.shape[1]
        lowrank = k[...] + g[...].astype(F32)
        new_first = 0.9 * first_ref[:, span] + 0.1 * lowrank
        new_second = 0.99 * second_ref[:, span] + 0.01 * lowrank * lowrank
        new_first_ref[:, span] = new_first
        new_second_ref[:, span] = new_second
        d[...] = (new_first / first_fix / (jnp.sqrt(new_second / second_fix) + 1e-08)).astype(
            d.dtype
        )


def adam(kept, got, first, second):
    outs = [shape(*first.shape, F32)] * 2 + [shape(*k.shape, BF) for k in kept]
    result = call(
        functools.partial(adam_kernel, len(kept)), outs, [*kept, *got, first, second]
    )
    return result[0], result[1], result[2:]


def early_kernel(count, *refs):
    factors, parts, out_ref = refs[:count], refs[count : 2 * count], refs[2 * count]
    at = 0
    for f, p in zip(factors, parts):
        depth, width = p.shape
        out_ref[:, at : at + width] = jnp.dot(
            f[:, :depth], p[...], preferred_element_type=F32
        )
        at += width


def late_kernel(count, row, *refs):
    factors, parts, sum_ref, out_ref = (
        refs[:count],
        refs[count : 2 * count],
        refs[2 * count],
        refs[2 * count + 1],
    )
    rows = out_ref.shape[0]
    at = 0
    for f, p in zip(factors, parts):
        depth, width = p.shape
        product = jnp.dot(f[row : row + rows, depth:], p[...], preferred_element_type=F32)
        out_ref[:, at : at + width] = (
            sum_ref[row : row + rows, at : at + width] + product
        ).astype(out_ref.dtype)
        at += width


def body(activations, grad_output, projector, first_moment, second_moment):
    place = lax.axis_index("fsdp").astype(jnp.int32)
    tp_place = lax.axis_index("tp").astype(jnp.int32)
    core = place & 1
    chip = place >> 1
    tokens, width = grad_output.shape
    half = width // 2
    rank = projector.shape[1]
    block = rank // 16
    column_count = rank // 8
    wide = half * 5 // 7
    widths = (wide, half - wide)
    rows = first_moment.shape[0]

    def my_half(array):
        return lax.dynamic_slice_in_dim(array, core * half, half, 1)

    def other_half(array):
        return lax.dynamic_slice_in_dim(array, (1 - core) * half, half, 1)

    columns = lax.dynamic_slice_in_dim(projector, tp_place * column_count, column_count, 1)
    column_orders = ([8, 24, 2, 6], [24, 8, 6, 2])
    for masks in zip(*column_orders):
        columns = stack([[columns, swap(columns, "fsdp", masks)]])[0]
    columns_other = swap_core(columns)
    order = [doubled(o) for o in column_orders]
    index = jnp.concatenate(
        [place ^ table(core, order), place ^ 1 ^ table(1 - core, order)]
    )
    act = reorder(activations, index, projector.shape[0])
    depth = columns.shape[0]
    dims = (((0,), (1,)), ((), ()))
    own = lax.dot_general(columns, act[:, :depth], dims, preferred_element_type=F32)
    own = own + lax.dot_general(columns_other, act[:, depth:], dims, preferred_element_type=F32)
    own = own.astype(BF)

    coords = own
    for masks in ((1, 1), (2, 6), (6, 2)):
        coords = stack([[coords, swap(coords, "tp", masks)]])[0]
    coords_other = swap_core(coords)

    def position(wanted, which):
        part = tp_place ^ (wanted >> 1)
        high = part >> 2
        mixed = ((part >> 1) ^ high) & 1
        upper = jnp.where(which == 0, 2 * mixed + 4 * high, 2 * high + 4 * mixed)
        return 2 * ((part & 1) + upper) + (wanted & 1)

    grads = jnp.concatenate(
        [my_half(grad_output), swap_core(other_half(grad_output))], axis=0
    )
    moments = jnp.concatenate([first_moment, second_moment], axis=0)
    moments_other = swap_core(other_half(moments))
    moments_own = my_half(moments)
    first = by_core(core, moments_own[:rows], moments_other[:rows], 0)
    second = by_core(core, moments_own[rows:], moments_other[rows:], 0)
    both = jnp.concatenate([projector, swap_core(projector)], axis=0)

    sum_orders = (([1, 3, 4, 12], [3, 1, 12, 4]), ([4, 12, 1, 3], [12, 4, 3, 1]))
    back_orders = [[o[::-1] for o in orders] for orders in sum_orders]
    keep_index, send_index = [], []
    for orders in sum_orders:
        wanted = chip ^ table(core, [doubled(o[::-1]) for o in orders])
        places = jnp.stack([position(wanted, core), position(wanted, 1 - core)])
        keep_index.append(places[:, :8])
        send_index.append(places[:, 8:])
    ranks = jnp.arange(rank, dtype=jnp.int32)
    factors = []
    for orders in back_orders:
        blocks = chip ^ table(core, [doubled(o) for o in orders])
        wanted = (blocks[:, None] * block + ranks[None, :block]).reshape(-1)
        choose = (ranks[:, None] == wanted[None, :]).astype(BF)
        factors.append(jnp.dot(both, choose, preferred_element_type=F32).astype(BF))

    def exchange(arrays, orders_of, stage):
        return [
            swap(a, "fsdp", [2 * o[stage] for o in orders]) for a, orders in zip(arrays, orders_of)
        ]

    arrays = (coords, coords_other, grads, rank // 2, widths, block)
    sent = partial_sums(jnp.concatenate(send_index, axis=1), *arrays, BF)
    kept = partial_sums(jnp.concatenate(keep_index, axis=1), *arrays, F32, after=factors)
    for stage in range(3):
        kept, sent = halve(kept, exchange(sent, sum_orders, stage))
    got = exchange(sent, sum_orders, 3)
    new_first, new_second, parts = adam(kept, got, first, second)

    def rows_of(array, which):
        return lax.dynamic_slice_in_dim(array, which * rows, rows, 0)

    states_other = swap_core(
        jnp.concatenate([rows_of(new_first, 1 - core), rows_of(new_second, 1 - core)], axis=0)
    )
    out_first = by_core(core, rows_of(new_first, core), states_other[:rows], 1)
    out_second = by_core(core, rows_of(new_second, core), states_other[rows:], 1)

    for stage in range(4):
        got = exchange(parts, back_orders, stage)
        if stage < 3:
            parts = stack([[p, g] for p, g in zip(parts, got)])
    count = len(parts)
    flops = rank * half * both.shape[0]
    early = call(
        functools.partial(early_kernel, count),
        [shape(both.shape[0], half, F32)],
        [*factors, *parts],
        flops=flops,
        vmem=12,
    )[0]
    late = [
        call(
            functools.partial(late_kernel, count, row),
            [shape(tokens, half, BF)],
            [*factors, *got, early],
            flops=flops // 2,
            vmem=12,
        )[0]
        for row in (tokens, 0)
    ]
    update = by_core(core, late[1], swap_core(late[0]), 1)
    return (out_first, out_second, update)


def solution(mesh):
    return jax.shard_map(
        body,
        mesh=mesh,
        in_specs=(
            P("fsdp", None),
            P("fsdp", "tp"),
            P("fsdp", None),
            P("fsdp", "tp"),
            P("fsdp", "tp"),
        ),
        out_specs=(P("fsdp", "tp"), P("fsdp", "tp"), P("fsdp", "tp")),
        check_vma=False,
    )
```

```python
import functools

import jax
import jax.numpy as jnp
from jax import lax
from jax.experimental import pallas as pl
from jax.experimental.pallas import tpu as pltpu
from jax.sharding import PartitionSpec as P

first_fix = 0.9999734386011124
second_fix = 0.6339676587267705
BF = jnp.bfloat16
F32 = jnp.float32
MIB = 2**20


def swap(array, axis, masks):
    inner = lax.axis_size("tp")
    count = lax.axis_size("fsdp") * inner
    scale = inner if axis == "fsdp" else 1
    return lax.ppermute(
        array, ("fsdp", "tp"), [(i, i ^ (scale * masks[i // inner % 2])) for i in range(count)]
    )


def swap_core(array):
    return swap(array, "fsdp", (1, 1))


def doubled(masks):
    order = [0]
    for mask in masks:
        order = order + [o ^ mask for o in order]
    return order


def table(core, orders):
    first, second = (jnp.array(order, dtype=jnp.int32) for order in orders)
    return jnp.where(core == 0, first, second)


def by_core(core, own, other, axis):
    return jnp.where(
        core == 0,
        jnp.concatenate([own, other], axis=axis),
        jnp.concatenate([other, own], axis=axis),
    )


def call(kernel, outs, args, flops=0, vmem=16, scratch=(), smem=0, after=()):
    moved = sum(a.size * a.dtype.itemsize for a in args)
    moved += sum(o.size * o.dtype.itemsize for o in outs)
    specs = [
        pl.BlockSpec(memory_space=pltpu.SMEM if i < smem else pltpu.VMEM)
        for i in range(len(args))
    ]
    count = len(args)

    def body(*refs):
        kernel(*refs[:count], *refs[count + len(after) :])

    specs += [pl.BlockSpec(memory_space=pl.ANY) for _ in after]
    return pl.pallas_call(
        body,
        out_shape=list(outs),
        in_specs=specs,
        out_specs=[pl.BlockSpec(memory_space=pltpu.VMEM) for _ in outs],
        scratch_shapes=list(scratch),
        compiler_params=pltpu.CompilerParams(vmem_limit_bytes=vmem * MIB),
        cost_estimate=pl.CostEstimate(flops=flops, bytes_accessed=moved, transcendentals=0),
    )(*args, *after)


def shape(rows, columns, kind):
    return jax.ShapeDtypeStruct((rows, columns), kind)


def stack_kernel(sizes, *refs):
    outs = refs[sum(sizes) :]
    at = 0
    for size, out_ref in zip(sizes, outs):
        row = 0
        for ref in refs[at : at + size]:
            out_ref[row : row + ref.shape[0], :] = ref[...]
            row += ref.shape[0]
        at += size


def stack(groups):
    outs = [shape(sum(a.shape[0] for a in g), g[0].shape[1], g[0].dtype) for g in groups]
    return call(
        functools.partial(stack_kernel, [len(g) for g in groups]),
        outs,
        [a for g in groups for a in g],
    )


def reorder_kernel(width, index_ref, in_ref, out_ref):
    for k in range(out_ref.shape[1] // width):
        start = pl.multiple_of(index_ref[k] * width, width)
        out_ref[:, k * width : (k + 1) * width] = in_ref[:, pl.ds(start, width)]


def reorder(array, index, width):
    outs = [shape(array.shape[0], array.shape[1], array.dtype)]
    return call(
        functools.partial(reorder_kernel, width), outs, [index, array], vmem=24, smem=1
    )[0]


def sums_kernel(count, block, index_ref, own_ref, other_ref, grads_ref, *refs):
    outs, chosen = refs[:count], refs[count]
    tokens = own_ref.shape[1]
    at = 0
    for part, out_ref in enumerate(outs):
        blocks = out_ref.shape[0] // block
        for k in range(blocks):
            row = slice(k * block, (k + 1) * block)
            start = pl.multiple_of(index_ref[part * blocks + k] * block, block)
            chosen[row, :tokens] = own_ref[pl.ds(start, block), :]
            chosen[row, tokens:] = other_ref[pl.ds(start, block), :]
        width = out_ref.shape[1]
        out_ref[...] = jnp.dot(
            chosen[...], grads_ref[:, at : at + width], preferred_element_type=F32
        ).astype(out_ref.dtype)
        at += width


def partial_sums(index, own, other, grads, rows, widths, block, kind, after=()):
    return call(
        functools.partial(sums_kernel, len(widths), block),
        [shape(rows, w, kind) for w in widths],
        [index, own, other, grads],
        flops=2 * rows * grads.size,
        vmem=24,
        scratch=[pltpu.VMEM((rows, 2 * own.shape[1]), BF)],
        smem=1,
        after=after,
    )


def halve_kernel(count, *refs):
    kept, got, kept_out, sent = (refs[i * count : (i + 1) * count] for i in range(4))
    for k, g, o, s in zip(kept, got, kept_out, sent):
        rows = o.shape[0]
        s[...] = (k[rows:, :] + g[rows:, :].astype(F32)).astype(s.dtype)
        o[...] = k[:rows, :] + g[:rows, :].astype(F32)


def halve(kept, got):
    rows = kept[0].shape[0] // 2
    outs = [shape(rows, k.shape[1], kind) for kind in (F32, BF) for k in kept]
    result = call(functools.partial(halve_kernel, len(kept)), outs, list(kept) + list(got))
    return result[: len(kept)], result[len(kept) :]


def adam_kernel(count, *refs):
    kept, got = refs[:count], refs[count : 2 * count]
    first_ref, second_ref = refs[2 * count : 2 * count + 2]
    new_first_ref, new_second_ref = refs[2 * count + 2 : 2 * count + 4]
    directions = refs[2 * count + 4 :]
    at = 0
    for k, g, d in zip(kept, got, directions):
        span = slice(at, at + k.shape[1])
        at += k.shape[1]
        lowrank = k[...] + g[...].astype(F32)
        new_first = 0.9 * first_ref[:, span] + 0.1 * lowrank
        new_second = 0.99 * second_ref[:, span] + 0.01 * lowrank * lowrank
        new_first_ref[:, span] = new_first
        new_second_ref[:, span] = new_second
        d[...] = (new_first / first_fix / (jnp.sqrt(new_second / second_fix) + 1e-08)).astype(
            d.dtype
        )


def adam(kept, got, first, second, after):
    outs = [shape(*first.shape, F32)] * 2 + [shape(*k.shape, BF) for k in kept]
    result = call(
        functools.partial(adam_kernel, len(kept)),
        outs,
        [*kept, *got, first, second],
        after=after,
    )
    return result[0], result[1], result[2:]


def pick_kernel(which_ref, first_ref, second_ref, out_ref):
    rows = out_ref.shape[0] // 2
    start = pl.multiple_of(which_ref[0] * rows, rows)
    out_ref[:rows, :] = first_ref[pl.ds(start, rows), :]
    out_ref[rows:, :] = second_ref[pl.ds(start, rows), :]


def early_kernel(count, *refs):
    factors, parts, out_ref = refs[:count], refs[count : 2 * count], refs[2 * count]
    at = 0
    for f, p in zip(factors, parts):
        depth, width = p.shape
        out_ref[:, at : at + width] = jnp.dot(
            f[:, :depth], p[...], preferred_element_type=F32
        )
        at += width


def late_kernel(count, row, *refs):
    factors, parts, sum_ref, out_ref = (
        refs[:count],
        refs[count : 2 * count],
        refs[2 * count],
        refs[2 * count + 1],
    )
    rows = out_ref.shape[0]
    at = 0
    for f, p in zip(factors, parts):
        depth, width = p.shape
        product = jnp.dot(f[row : row + rows, depth:], p[...], preferred_element_type=F32)
        out_ref[:, at : at + width] = (
            sum_ref[row : row + rows, at : at + width] + product
        ).astype(out_ref.dtype)
        at += width


def body(activations, grad_output, projector, first_moment, second_moment):
    place = lax.axis_index("fsdp").astype(jnp.int32)
    tp_place = lax.axis_index("tp").astype(jnp.int32)
    core = place & 1
    chip = place >> 1
    tokens, width = grad_output.shape
    half = width // 2
    rank = projector.shape[1]
    block = rank // 16
    column_count = rank // 8
    wide = half * 5 // 14
    widths = (wide, wide, half - 2 * wide)
    rows = first_moment.shape[0]

    def my_half(array):
        return lax.dynamic_slice_in_dim(array, core * half, half, 1)

    def other_half(array):
        return lax.dynamic_slice_in_dim(array, (1 - core) * half, half, 1)

    columns = lax.dynamic_slice_in_dim(projector, tp_place * column_count, column_count, 1)
    for masks in ((8, 16, 24), (2, 4, 6)):
        columns = stack([[columns] + [swap(columns, "fsdp", (m, m)) for m in masks]])[0]
    columns_other = swap_core(columns)
    order = jnp.array([x + z for x in (0, 2, 4, 6) for z in (0, 8, 16, 24)], jnp.int32)
    index = jnp.concatenate([place ^ order, place ^ 1 ^ order])
    act = reorder(activations, index, projector.shape[0])
    depth = columns.shape[0]
    dims = (((0,), (1,)), ((), ()))
    own = lax.dot_general(columns, act[:, :depth], dims, preferred_element_type=F32)
    own = own + lax.dot_general(columns_other, act[:, depth:], dims, preferred_element_type=F32)
    own = own.astype(BF)

    coords = stack([[own, swap(own, "tp", (1, 1))]])[0]
    coords = stack([[coords] + [swap(coords, "tp", (m, m)) for m in (2, 4, 6)]])[0]
    coords_other = swap_core(coords)

    grads = jnp.concatenate(
        [my_half(grad_output), swap_core(other_half(grad_output))], axis=0
    )
    moments = jnp.concatenate([first_moment, second_moment], axis=0)
    moments_other = swap_core(other_half(moments))
    moments_own = my_half(moments)
    first = by_core(core, moments_own[:rows], moments_other[:rows], 0)
    second = by_core(core, moments_own[rows:], moments_other[rows:], 0)
    both = jnp.concatenate([projector, swap_core(projector)], axis=0)

    sum_orders = (
        ([1, 3, 4, 12], [1, 3, 4, 12]),
        ([3, 1, 12, 4], [3, 1, 12, 4]),
        ([4, 12, 1, 3], [12, 4, 3, 1]),
    )
    back_orders = [[o[::-1] for o in orders] for orders in sum_orders]
    keep_index, send_index = [], []
    for orders in sum_orders:
        wanted = chip ^ table(core, [doubled(o[::-1]) for o in orders])
        position = 2 * (tp_place ^ (wanted >> 1)) + (wanted & 1)
        keep_index.append(position[:8])
        send_index.append(position[8:])
    ranks = jnp.arange(rank, dtype=jnp.int32)
    factors = []
    for orders in back_orders:
        blocks = chip ^ table(core, [doubled(o) for o in orders])
        wanted = (blocks[:, None] * block + ranks[None, :block]).reshape(-1)
        choose = (ranks[:, None] == wanted[None, :]).astype(BF)
        factors.append(jnp.dot(both, choose, preferred_element_type=F32).astype(BF))

    def exchange(arrays, orders_of, stage):
        return [
            swap(a, "fsdp", [2 * o[stage] for o in orders]) for a, orders in zip(arrays, orders_of)
        ]

    arrays = (coords, coords_other, grads, rank // 2, widths, block)
    sent = partial_sums(jnp.concatenate(send_index), *arrays, BF)
    kept = partial_sums(jnp.concatenate(keep_index), *arrays, F32)
    for stage in range(3):
        kept, sent = halve(kept, exchange(sent, sum_orders, stage))
    got = exchange(sent, sum_orders, 3)
    new_first, new_second, parts = adam(kept, got, first, second, factors)

    def rows_of(array, which):
        return lax.dynamic_slice_in_dim(array, which * rows, rows, 0)

    for stage in range(4):
        got = exchange(parts, back_orders, stage)
        if stage < 3:
            parts = stack([[p, g] for p, g in zip(parts, got)])
    count = len(parts)
    flops = rank * half * both.shape[0]
    early = call(
        functools.partial(early_kernel, count),
        [shape(both.shape[0], half, F32)],
        [*factors, *parts],
        flops=flops,
        vmem=32,
    )[0]
    late = [
        call(
            functools.partial(late_kernel, count, row),
            [shape(tokens, half, BF)],
            [*factors, *got, early],
            flops=flops // 2,
            vmem=32,
        )[0]
        for row in (tokens, 0)
    ]
    late_other = swap_core(late[0])
    states_other = swap_core(
        call(
            pick_kernel,
            [shape(2 * rows, half, F32)],
            [(1 - core)[None], new_first, new_second],
            smem=1,
            after=[late[0]],
        )[0]
    )
    out_first = by_core(core, rows_of(new_first, core), states_other[:rows], 1)
    out_second = by_core(core, rows_of(new_second, core), states_other[rows:], 1)
    update = by_core(core, late[1], late_other, 1)
    return (out_first, out_second, update)


def solution(mesh):
    return jax.shard_map(
        body,
        mesh=mesh,
        in_specs=(
            P("fsdp", None),
            P("fsdp", "tp"),
            P("fsdp", None),
            P("fsdp", "tp"),
            P("fsdp", "tp"),
        ),
        out_specs=(P("fsdp", "tp"), P("fsdp", "tp"), P("fsdp", "tp")),
        check_vma=False,
    )
```

```python
import functools

import jax
import jax.numpy as jnp
from jax import lax
from jax.experimental import pallas as pl
from jax.experimental.pallas import tpu as pltpu
from jax.sharding import PartitionSpec as P

first_fix = 0.9999734386011124
second_fix = 0.6339676587267705
BF = jnp.bfloat16
F32 = jnp.float32
MIB = 2**20


def swap(array, axis, masks):
    inner = lax.axis_size("tp")
    count = lax.axis_size("fsdp") * inner
    scale = inner if axis == "fsdp" else 1
    return lax.ppermute(
        array, ("fsdp", "tp"), [(i, i ^ (scale * masks[i // inner % 2])) for i in range(count)]
    )


def swap_core(array):
    return swap(array, "fsdp", (1, 1))


def doubled(masks):
    order = [0]
    for mask in masks:
        order = order + [o ^ mask for o in order]
    return order


def table(core, orders):
    first, second = (jnp.array(order, dtype=jnp.int32) for order in orders)
    return jnp.where(core == 0, first, second)


def by_core(core, own, other, axis):
    return jnp.where(
        core == 0,
        jnp.concatenate([own, other], axis=axis),
        jnp.concatenate([other, own], axis=axis),
    )


def call(kernel, outs, args, flops=0, vmem=8, scratch=(), smem=0, after=()):
    moved = sum(a.size * a.dtype.itemsize for a in args)
    moved += sum(o.size * o.dtype.itemsize for o in outs)
    specs = [
        pl.BlockSpec(memory_space=pltpu.SMEM if i < smem else pltpu.VMEM)
        for i in range(len(args))
    ]
    count = len(args)

    def body(*refs):
        kernel(*refs[:count], *refs[count + len(after) :])

    specs += [pl.BlockSpec(memory_space=pl.ANY) for _ in after]
    return pl.pallas_call(
        body,
        out_shape=list(outs),
        in_specs=specs,
        out_specs=[pl.BlockSpec(memory_space=pltpu.VMEM) for _ in outs],
        scratch_shapes=list(scratch),
        compiler_params=pltpu.CompilerParams(vmem_limit_bytes=vmem * MIB),
        cost_estimate=pl.CostEstimate(flops=flops, bytes_accessed=moved, transcendentals=0),
    )(*args, *after)


def shape(rows, columns, kind):
    return jax.ShapeDtypeStruct((rows, columns), kind)


def with_mark(kernel):
    def body(*refs):
        refs[-1][...] = jnp.zeros(refs[-1].shape, refs[-1].dtype)
        kernel(*refs[:-1])

    return body


def stack_kernel(sizes, *refs):
    outs = refs[sum(sizes) :]
    at = 0
    for size, out_ref in zip(sizes, outs):
        row = 0
        for ref in refs[at : at + size]:
            out_ref[row : row + ref.shape[0], :] = ref[...]
            row += ref.shape[0]
        at += size


def stack(groups):
    outs = [shape(sum(a.shape[0] for a in g), g[0].shape[1], g[0].dtype) for g in groups]
    return call(
        functools.partial(stack_kernel, [len(g) for g in groups]),
        outs,
        [a for g in groups for a in g],
    )


def stack_marked(groups, after):
    outs = [shape(sum(a.shape[0] for a in g), g[0].shape[1], g[0].dtype) for g in groups]
    *result, mark = call(
        with_mark(functools.partial(stack_kernel, [len(g) for g in groups])),
        [*outs, shape(8, 128, F32)],
        [a for g in groups for a in g],
        after=after,
    )
    return result, mark


def reorder_kernel(width, index_ref, in_ref, out_ref):
    for k in range(out_ref.shape[1] // width):
        start = pl.multiple_of(index_ref[k] * width, width)
        out_ref[:, k * width : (k + 1) * width] = in_ref[:, pl.ds(start, width)]


def reorder(array, index, width):
    outs = [shape(array.shape[0], array.shape[1], array.dtype)]
    return call(
        functools.partial(reorder_kernel, width), outs, [index, array], vmem=8, smem=1
    )[0]


def sums_kernel(count, block, index_ref, own_ref, other_ref, grads_ref, *refs):
    outs, chosen = refs[:count], refs[count]
    tokens = own_ref.shape[1]
    at = 0
    for part, out_ref in enumerate(outs):
        blocks = out_ref.shape[0] // block
        for k in range(blocks):
            row = slice(k * block, (k + 1) * block)
            start = pl.multiple_of(index_ref[part * blocks + k] * block, block)
            chosen[row, :tokens] = own_ref[pl.ds(start, block), :]
            chosen[row, tokens:] = other_ref[pl.ds(start, block), :]
        width = out_ref.shape[1]
        out_ref[...] = jnp.dot(
            chosen[...], grads_ref[:, at : at + width], preferred_element_type=F32
        ).astype(out_ref.dtype)
        at += width


def partial_sums(index, own, other, grads, rows, widths, block, kind, after=()):
    return call(
        functools.partial(sums_kernel, len(widths), block),
        [shape(rows, w, kind) for w in widths],
        [index, own, other, grads],
        flops=2 * rows * grads.size,
        vmem=8,
        scratch=[pltpu.VMEM((rows, 2 * own.shape[1]), BF)],
        smem=1,
        after=after,
    )


def halve_kernel(count, *refs):
    kept, got, kept_out, sent = (refs[i * count : (i + 1) * count] for i in range(4))
    for k, g, o, s in zip(kept, got, kept_out, sent):
        rows = o.shape[0]
        s[...] = (k[rows:, :] + g[rows:, :].astype(F32)).astype(s.dtype)
        o[...] = k[:rows, :] + g[:rows, :].astype(F32)


def halve(kept, got, after):
    rows = kept[0].shape[0] // 2
    outs = [shape(rows, k.shape[1], kind) for kind in (F32, BF) for k in kept]
    *result, mark = call(
        with_mark(functools.partial(halve_kernel, len(kept))),
        [*outs, shape(8, 128, F32)],
        [*kept, *got],
        after=after,
    )
    return result[: len(kept)], result[len(kept) :], mark


def adam_kernel(count, *refs):
    kept, got = refs[:count], refs[count : 2 * count]
    first_ref, second_ref = refs[2 * count : 2 * count + 2]
    new_first_ref, new_second_ref = refs[2 * count + 2 : 2 * count + 4]
    directions = refs[2 * count + 4 :]
    at = 0
    for k, g, d in zip(kept, got, directions):
        span = slice(at, at + k.shape[1])
        at += k.shape[1]
        lowrank = k[...] + g[...].astype(F32)
        new_first = 0.9 * first_ref[:, span] + 0.1 * lowrank
        new_second = 0.99 * second_ref[:, span] + 0.01 * lowrank * lowrank
        new_first_ref[:, span] = new_first
        new_second_ref[:, span] = new_second
        d[...] = (new_first / first_fix / (jnp.sqrt(new_second / second_fix) + 1e-08)).astype(
            d.dtype
        )


def adam(kept, got, first, second, after):
    outs = [shape(*first.shape, F32)] * 2 + [shape(*k.shape, BF) for k in kept]
    result = call(
        functools.partial(adam_kernel, len(kept)),
        outs,
        [*kept, *got, first, second],
        after=after,
    )
    return result[0], result[1], result[2:]


def pick_kernel(which_ref, first_ref, second_ref, out_ref):
    rows = out_ref.shape[0] // 2
    start = pl.multiple_of(which_ref[0] * rows, rows)
    out_ref[:rows, :] = first_ref[pl.ds(start, rows), :]
    out_ref[rows:, :] = second_ref[pl.ds(start, rows), :]


def join_kernel(core_ref, first_ref, second_ref, other_ref, out_first_ref, out_second_ref):
    rows, half = out_first_ref.shape[0], first_ref.shape[1]
    core = core_ref[0]
    start = pl.multiple_of(core * rows, rows)
    own = pl.ds(pl.multiple_of(core * half, half), half)
    other = pl.ds(pl.multiple_of((1 - core) * half, half), half)
    out_first_ref[:, own] = first_ref[pl.ds(start, rows), :]
    out_first_ref[:, other] = other_ref[:rows, :]
    out_second_ref[:, own] = second_ref[pl.ds(start, rows), :]
    out_second_ref[:, other] = other_ref[rows:, :]


def early_kernel(count, *refs):
    factors, parts, out_ref = refs[:count], refs[count : 2 * count], refs[2 * count]
    at = 0
    for f, p in zip(factors, parts):
        depth, width = p.shape
        out_ref[:, at : at + width] = jnp.dot(
            f[:, :depth], p[...], preferred_element_type=F32
        )
        at += width


def late_kernel(count, row, *refs):
    factors, parts, sum_ref, out_ref = (
        refs[:count],
        refs[count : 2 * count],
        refs[2 * count],
        refs[2 * count + 1],
    )
    rows = out_ref.shape[0]
    at = 0
    for f, p in zip(factors, parts):
        depth, width = p.shape
        product = jnp.dot(f[row : row + rows, depth:], p[...], preferred_element_type=F32)
        out_ref[:, at : at + width] = (
            sum_ref[row : row + rows, at : at + width] + product
        ).astype(out_ref.dtype)
        at += width


def body(activations, grad_output, projector, first_moment, second_moment):
    place = lax.axis_index("fsdp").astype(jnp.int32)
    tp_place = lax.axis_index("tp").astype(jnp.int32)
    core = place & 1
    chip = place >> 1
    tokens, width = grad_output.shape
    half = width // 2
    rank = projector.shape[1]
    block = rank // 16
    column_count = rank // 8
    wide = half * 5 // 14
    widths = (wide, wide, half - 2 * wide)
    rows = first_moment.shape[0]

    def my_half(array):
        return lax.dynamic_slice_in_dim(array, core * half, half, 1)

    def other_half(array):
        return lax.dynamic_slice_in_dim(array, (1 - core) * half, half, 1)

    columns = lax.dynamic_slice_in_dim(projector, tp_place * column_count, column_count, 1)
    for masks in ((8, 16, 24), (2, 4, 6)):
        columns = stack([[columns] + [swap(columns, "fsdp", (m, m)) for m in masks]])[0]
    columns_other = swap_core(columns)
    order = jnp.array([x + z for x in (0, 2, 4, 6) for z in (0, 8, 16, 24)], jnp.int32)
    index = jnp.concatenate([place ^ order, place ^ 1 ^ order])
    act = reorder(activations, index, projector.shape[0])
    depth = columns.shape[0]
    dims = (((0,), (1,)), ((), ()))
    own = lax.dot_general(columns, act[:, :depth], dims, preferred_element_type=F32)
    own = own + lax.dot_general(columns_other, act[:, depth:], dims, preferred_element_type=F32)
    own = own.astype(BF)

    coords = stack([[own, swap(own, "tp", (1, 1))]])[0]
    coords = stack([[coords] + [swap(coords, "tp", (m, m)) for m in (2, 4, 6)]])[0]
    coords_other = swap_core(coords)

    grads = jnp.concatenate(
        [my_half(grad_output), swap_core(other_half(grad_output))], axis=0
    )
    moments = jnp.concatenate([first_moment, second_moment], axis=0)
    moments_other = swap_core(other_half(moments))
    moments_own = my_half(moments)
    first = by_core(core, moments_own[:rows], moments_other[:rows], 0)
    second = by_core(core, moments_own[rows:], moments_other[rows:], 0)
    both = jnp.concatenate([projector, swap_core(projector)], axis=0)

    sum_orders = (
        ([1, 3, 4, 12], [1, 3, 4, 12]),
        ([3, 1, 12, 4], [3, 1, 12, 4]),
        ([4, 12, 1, 3], [12, 4, 3, 1]),
    )
    back_orders = [[o[::-1] for o in orders] for orders in sum_orders]
    keep_index, send_index = [], []
    for orders in sum_orders:
        wanted = chip ^ table(core, [doubled(o[::-1]) for o in orders])
        position = 2 * (tp_place ^ (wanted >> 1)) + (wanted & 1)
        keep_index.append(position[:8])
        send_index.append(position[8:])
    ranks = jnp.arange(rank, dtype=jnp.int32)
    factors = []
    for orders in back_orders:
        blocks = chip ^ table(core, [doubled(o) for o in orders])
        wanted = (blocks[:, None] * block + ranks[None, :block]).reshape(-1)
        choose = (ranks[:, None] == wanted[None, :]).astype(BF)
        factors.append(jnp.dot(both, choose, preferred_element_type=F32).astype(BF))

    def exchange(arrays, orders_of, stage):
        return [
            swap(a, "fsdp", [2 * o[stage] for o in orders]) for a, orders in zip(arrays, orders_of)
        ]

    arrays = (coords, coords_other, grads, rank // 2, widths, block)
    sent = partial_sums(jnp.concatenate(send_index), *arrays, BF, after=[both])
    kept = partial_sums(jnp.concatenate(keep_index), *arrays, F32)
    marks = []
    for stage in range(3):
        kept, sent, mark = halve(kept, exchange(sent, sum_orders, stage), marks)
        marks = [swap_core(mark)]
    got = exchange(sent, sum_orders, 3)
    new_first, new_second, parts = adam(kept, got, first, second, [*factors, *marks])

    states_other = swap_core(
        call(
            pick_kernel,
            [shape(2 * rows, half, F32)],
            [(1 - core)[None], new_first, new_second],
            smem=1,
        )[0]
    )
    out_first, out_second, joined = call(
        with_mark(join_kernel),
        [shape(rows, width, F32)] * 2 + [shape(8, 128, F32)],
        [core[None], new_first, new_second, states_other],
        smem=1,
    )
    marks = [states_other]
    for stage in range(4):
        got = exchange(parts, back_orders, stage)
        if stage == 1:
            marks = [*marks, joined]
        if stage < 3:
            parts, mark = stack_marked([[p, g] for p, g in zip(parts, got)], marks)
            marks = [swap_core(mark)]
    count = len(parts)
    flops = rank * half * both.shape[0]
    early = call(
        functools.partial(early_kernel, count),
        [shape(both.shape[0], half, F32)],
        [*factors, *parts],
        flops=flops,
        vmem=8,
        after=marks,
    )[0]
    late = [
        call(
            functools.partial(late_kernel, count, row),
            [shape(tokens, half, BF)],
            [*factors, *got, early],
            flops=flops // 2,
            vmem=8,
        )[0]
        for row in (tokens, 0)
    ]
    late_other = swap_core(late[0])
    update = by_core(core, late[1], late_other, 1)
    return (out_first, out_second, update)


def solution(mesh):
    return jax.shard_map(
        body,
        mesh=mesh,
        in_specs=(
            P("fsdp", None),
            P("fsdp", "tp"),
            P("fsdp", None),
            P("fsdp", "tp"),
            P("fsdp", "tp"),
        ),
        out_specs=(P("fsdp", "tp"), P("fsdp", "tp"), P("fsdp", "tp")),
        check_vma=False,
    )
```

```python
import functools

import jax
import jax.numpy as jnp
from jax import lax
from jax.experimental import pallas as pl
from jax.experimental.pallas import tpu as pltpu
from jax.sharding import PartitionSpec as P

first_fix = 0.9999734386011124
second_fix = 0.6339676587267705
BF = jnp.bfloat16
F32 = jnp.float32
MIB = 2**20


def swap(array, axis, masks):
    inner = lax.axis_size("tp")
    count = lax.axis_size("fsdp") * inner
    scale = inner if axis == "fsdp" else 1
    return lax.ppermute(
        array, ("fsdp", "tp"), [(i, i ^ (scale * masks[i // inner % 2])) for i in range(count)]
    )


def swap_core(array):
    return swap(array, "fsdp", (1, 1))


def doubled(masks):
    order = [0]
    for mask in masks:
        order = order + [o ^ mask for o in order]
    return order


def table(core, orders):
    first, second = (jnp.array(order, dtype=jnp.int32) for order in orders)
    return jnp.where(core == 0, first, second)


def by_core(core, own, other, axis):
    return jnp.where(
        core == 0,
        jnp.concatenate([own, other], axis=axis),
        jnp.concatenate([other, own], axis=axis),
    )


def call(kernel, outs, args, flops=0, vmem=8, scratch=(), smem=0, after=()):
    moved = sum(a.size * a.dtype.itemsize for a in args)
    moved += sum(o.size * o.dtype.itemsize for o in outs)
    specs = [
        pl.BlockSpec(memory_space=pltpu.SMEM if i < smem else pltpu.VMEM)
        for i in range(len(args))
    ]
    count = len(args)

    def body(*refs):
        kernel(*refs[:count], *refs[count + len(after) :])

    specs += [pl.BlockSpec(memory_space=pl.ANY) for _ in after]
    return pl.pallas_call(
        body,
        out_shape=list(outs),
        in_specs=specs,
        out_specs=[pl.BlockSpec(memory_space=pltpu.VMEM) for _ in outs],
        scratch_shapes=list(scratch),
        compiler_params=pltpu.CompilerParams(vmem_limit_bytes=vmem * MIB),
        cost_estimate=pl.CostEstimate(flops=flops, bytes_accessed=moved, transcendentals=0),
    )(*args, *after)


def shape(rows, columns, kind):
    return jax.ShapeDtypeStruct((rows, columns), kind)


def with_mark(kernel):
    def body(*refs):
        refs[-1][...] = jnp.zeros(refs[-1].shape, refs[-1].dtype)
        kernel(*refs[:-1])

    return body


def stack_kernel(sizes, *refs):
    outs = refs[sum(sizes) :]
    at = 0
    for size, out_ref in zip(sizes, outs):
        row = 0
        for ref in refs[at : at + size]:
            out_ref[row : row + ref.shape[0], :] = ref[...]
            row += ref.shape[0]
        at += size


def stack(groups):
    outs = [shape(sum(a.shape[0] for a in g), g[0].shape[1], g[0].dtype) for g in groups]
    return call(
        functools.partial(stack_kernel, [len(g) for g in groups]),
        outs,
        [a for g in groups for a in g],
    )


def stack_marked(groups, after):
    outs = [shape(sum(a.shape[0] for a in g), g[0].shape[1], g[0].dtype) for g in groups]
    *result, mark = call(
        with_mark(functools.partial(stack_kernel, [len(g) for g in groups])),
        [*outs, shape(8, 128, F32)],
        [a for g in groups for a in g],
        after=after,
    )
    return result, mark


def reorder_kernel(width, index_ref, in_ref, out_ref):
    for k in range(out_ref.shape[1] // width):
        start = pl.multiple_of(index_ref[k] * width, width)
        out_ref[:, k * width : (k + 1) * width] = in_ref[:, pl.ds(start, width)]


def reorder(array, index, width):
    outs = [shape(array.shape[0], array.shape[1], array.dtype)]
    return call(
        functools.partial(reorder_kernel, width), outs, [index, array], vmem=8, smem=1
    )[0]


def sums_kernel(count, block, index_ref, own_ref, other_ref, grads_ref, *refs):
    outs, chosen = refs[:count], refs[count]
    tokens = own_ref.shape[1]
    at = 0
    for part, out_ref in enumerate(outs):
        blocks = out_ref.shape[0] // block
        for k in range(blocks):
            row = slice(k * block, (k + 1) * block)
            start = pl.multiple_of(index_ref[part * blocks + k] * block, block)
            chosen[row, :tokens] = own_ref[pl.ds(start, block), :]
            chosen[row, tokens:] = other_ref[pl.ds(start, block), :]
        width = out_ref.shape[1]
        out_ref[...] = jnp.dot(
            chosen[...], grads_ref[:, at : at + width], preferred_element_type=F32
        ).astype(out_ref.dtype)
        at += width


def partial_sums(index, own, other, grads, rows, widths, block, kind, after=()):
    return call(
        functools.partial(sums_kernel, len(widths), block),
        [shape(rows, w, kind) for w in widths],
        [index, own, other, grads],
        flops=2 * rows * grads.size,
        vmem=8,
        scratch=[pltpu.VMEM((rows, 2 * own.shape[1]), BF)],
        smem=1,
        after=after,
    )


def halve_kernel(count, *refs):
    kept, got, kept_out, sent = (refs[i * count : (i + 1) * count] for i in range(4))
    for k, g, o, s in zip(kept, got, kept_out, sent):
        rows = o.shape[0]
        s[...] = (k[rows:, :] + g[rows:, :].astype(F32)).astype(s.dtype)
        o[...] = k[:rows, :] + g[:rows, :].astype(F32)


def halve(kept, got, after):
    rows = kept[0].shape[0] // 2
    outs = [shape(rows, k.shape[1], kind) for kind in (F32, BF) for k in kept]
    *result, mark = call(
        with_mark(functools.partial(halve_kernel, len(kept))),
        [*outs, shape(8, 128, F32)],
        [*kept, *got],
        after=after,
    )
    return result[: len(kept)], result[len(kept) :], mark


def adam_kernel(count, *refs):
    kept, got = refs[:count], refs[count : 2 * count]
    first_ref, second_ref = refs[2 * count : 2 * count + 2]
    new_first_ref, new_second_ref = refs[2 * count + 2 : 2 * count + 4]
    directions = refs[2 * count + 4 :]
    at = 0
    for k, g, d in zip(kept, got, directions):
        span = slice(at, at + k.shape[1])
        at += k.shape[1]
        lowrank = k[...] + g[...].astype(F32)
        new_first = 0.9 * first_ref[:, span] + 0.1 * lowrank
        new_second = 0.99 * second_ref[:, span] + 0.01 * lowrank * lowrank
        new_first_ref[:, span] = new_first
        new_second_ref[:, span] = new_second
        d[...] = (new_first / first_fix / (jnp.sqrt(new_second / second_fix) + 1e-08)).astype(
            d.dtype
        )


def adam(kept, got, first, second, after):
    outs = [shape(*first.shape, F32)] * 2 + [shape(*k.shape, BF) for k in kept]
    result = call(
        functools.partial(adam_kernel, len(kept)),
        outs,
        [*kept, *got, first, second],
        after=after,
    )
    return result[0], result[1], result[2:]


def pick_kernel(which_ref, first_ref, second_ref, out_ref):
    rows = out_ref.shape[0] // 2
    start = pl.multiple_of(which_ref[0] * rows, rows)
    out_ref[:rows, :] = first_ref[pl.ds(start, rows), :]
    out_ref[rows:, :] = second_ref[pl.ds(start, rows), :]


def join_kernel(core_ref, first_ref, second_ref, other_ref, out_first_ref, out_second_ref):
    rows, half = out_first_ref.shape[0], first_ref.shape[1]
    core = core_ref[0]
    start = pl.multiple_of(core * rows, rows)
    own = pl.ds(pl.multiple_of(core * half, half), half)
    other = pl.ds(pl.multiple_of((1 - core) * half, half), half)
    out_first_ref[:, own] = first_ref[pl.ds(start, rows), :]
    out_first_ref[:, other] = other_ref[:rows, :]
    out_second_ref[:, own] = second_ref[pl.ds(start, rows), :]
    out_second_ref[:, other] = other_ref[rows:, :]


def early_kernel(count, *refs):
    factors, parts, out_ref = refs[:count], refs[count : 2 * count], refs[2 * count]
    at = 0
    for f, p in zip(factors, parts):
        depth, width = p.shape
        out_ref[:, at : at + width] = jnp.dot(
            f[:, :depth], p[...], preferred_element_type=F32
        )
        at += width


def late_kernel(count, row, at, *refs):
    factors, parts, sum_ref, out_ref = (
        refs[:count],
        refs[count : 2 * count],
        refs[2 * count],
        refs[2 * count + 1],
    )
    rows = out_ref.shape[0]
    to = 0
    for f, p in zip(factors, parts):
        depth, width = p.shape
        product = jnp.dot(f[row : row + rows, depth:], p[...], preferred_element_type=F32)
        out_ref[:, to : to + width] = (
            sum_ref[row : row + rows, at : at + width] + product
        ).astype(out_ref.dtype)
        at += width
        to += width


def body(activations, grad_output, projector, first_moment, second_moment):
    place = lax.axis_index("fsdp").astype(jnp.int32)
    tp_place = lax.axis_index("tp").astype(jnp.int32)
    core = place & 1
    chip = place >> 1
    tokens, width = grad_output.shape
    half = width // 2
    rank = projector.shape[1]
    block = rank // 16
    column_count = rank // 8
    wide, middle = half * 3 // 7, half * 5 // 14
    widths = (wide, middle, half - wide - middle)
    rows = first_moment.shape[0]

    def my_half(array):
        return lax.dynamic_slice_in_dim(array, core * half, half, 1)

    def other_half(array):
        return lax.dynamic_slice_in_dim(array, (1 - core) * half, half, 1)

    columns = lax.dynamic_slice_in_dim(projector, tp_place * column_count, column_count, 1)
    for masks in ((8, 16, 24), (2, 4, 6)):
        columns = stack([[columns] + [swap(columns, "fsdp", (m, m)) for m in masks]])[0]
    columns_other = swap_core(columns)
    order = jnp.array([x + z for x in (0, 2, 4, 6) for z in (0, 8, 16, 24)], jnp.int32)
    index = jnp.concatenate([place ^ order, place ^ 1 ^ order])
    act = reorder(activations, index, projector.shape[0])
    depth = columns.shape[0]
    dims = (((0,), (1,)), ((), ()))
    own = lax.dot_general(columns, act[:, :depth], dims, preferred_element_type=F32)
    own = own + lax.dot_general(columns_other, act[:, depth:], dims, preferred_element_type=F32)
    own = own.astype(BF)

    coords = stack([[own, swap(own, "tp", (1, 1))]])[0]
    coords = stack([[coords] + [swap(coords, "tp", (m, m)) for m in (2, 4, 6)]])[0]
    coords_other = swap_core(coords)

    grads = jnp.concatenate(
        [my_half(grad_output), swap_core(other_half(grad_output))], axis=0
    )
    moments = jnp.concatenate([first_moment, second_moment], axis=0)
    moments_other = swap_core(other_half(moments))
    moments_own = my_half(moments)
    first = by_core(core, moments_own[:rows], moments_other[:rows], 0)
    second = by_core(core, moments_own[rows:], moments_other[rows:], 0)
    both = jnp.concatenate([projector, swap_core(projector)], axis=0)

    sum_orders = (
        ([1, 3, 4, 12], [3, 1, 12, 4]),
        ([3, 1, 12, 4], [1, 3, 4, 12]),
        ([4, 12, 1, 3], [12, 4, 3, 1]),
    )
    back_orders = [[o[::-1] for o in orders] for orders in sum_orders]
    keep_index, send_index = [], []
    for orders in sum_orders:
        wanted = chip ^ table(core, [doubled(o[::-1]) for o in orders])
        position = 2 * (tp_place ^ (wanted >> 1)) + (wanted & 1)
        keep_index.append(position[:8])
        send_index.append(position[8:])
    ranks = jnp.arange(rank, dtype=jnp.int32)
    factors = []
    for orders in back_orders:
        blocks = chip ^ table(core, [doubled(o) for o in orders])
        wanted = (blocks[:, None] * block + ranks[None, :block]).reshape(-1)
        choose = (ranks[:, None] == wanted[None, :]).astype(BF)
        factors.append(jnp.dot(both, choose, preferred_element_type=F32).astype(BF))

    def exchange(arrays, orders_of, stage):
        return [
            swap(a, "fsdp", [2 * o[stage] for o in orders]) for a, orders in zip(arrays, orders_of)
        ]

    arrays = (coords, coords_other, grads, rank // 2, widths, block)
    sent = partial_sums(jnp.concatenate(send_index), *arrays, BF)
    kept = partial_sums(jnp.concatenate(keep_index), *arrays, F32)
    marks = []
    for stage in range(3):
        kept, sent, mark = halve(kept, exchange(sent, sum_orders, stage), marks)
        marks = [swap_core(mark)]
    got = exchange(sent, sum_orders, 3)
    new_first, new_second, parts = adam(kept, got, first, second, [*factors, *marks])

    states_other = swap_core(
        call(
            pick_kernel,
            [shape(2 * rows, half, F32)],
            [(1 - core)[None], new_first, new_second],
            smem=1,
        )[0]
    )
    out_first, out_second, joined = call(
        with_mark(join_kernel),
        [shape(rows, width, F32)] * 2 + [shape(8, 128, F32)],
        [core[None], new_first, new_second, states_other],
        smem=1,
    )
    marks = [states_other]
    for stage in range(4):
        got = exchange(parts, back_orders, stage)
        if stage == 1:
            marks = [*marks, joined]
        if stage < 3:
            parts, mark = stack_marked([[p, g] for p, g in zip(parts, got)], marks)
            marks = [swap_core(mark)]
    count = len(parts)
    flops = rank * half * both.shape[0]
    early = call(
        functools.partial(early_kernel, count),
        [shape(both.shape[0], half, F32)],
        [*factors, *parts],
        flops=flops,
        vmem=8,
        after=marks,
    )[0]

    def late(row, parts, after=()):
        at = sum(widths[: parts.start])
        span = sum(widths[parts])
        return call(
            functools.partial(late_kernel, len(widths[parts]), row, at),
            [shape(tokens, span, BF)],
            [*factors[parts], *got[parts], early],
            flops=rank * tokens * span,
            after=after,
        )[0]

    every = slice(0, count)
    other = swap_core(late(tokens, every))
    update = by_core(core, late(0, every), other, 1)
    return (out_first, out_second, update)


def solution(mesh):
    return jax.shard_map(
        body,
        mesh=mesh,
        in_specs=(
            P("fsdp", None),
            P("fsdp", "tp"),
            P("fsdp", None),
            P("fsdp", "tp"),
            P("fsdp", "tp"),
        ),
        out_specs=(P("fsdp", "tp"), P("fsdp", "tp"), P("fsdp", "tp")),
        check_vma=False,
    )
```

```python
import functools

import jax
import jax.numpy as jnp
from jax import lax
from jax.experimental import pallas as pl
from jax.experimental.pallas import tpu as pltpu
from jax.sharding import PartitionSpec as P

first_fix = 0.9999734386011124
second_fix = 0.6339676587267705
BF = jnp.bfloat16
F32 = jnp.float32
MIB = 2**20


def swap(array, axis, masks):
    inner = lax.axis_size("tp")
    count = lax.axis_size("fsdp") * inner
    scale = inner if axis == "fsdp" else 1
    return lax.ppermute(
        array, ("fsdp", "tp"), [(i, i ^ (scale * masks[i // inner % 2])) for i in range(count)]
    )


def swap_core(array):
    return swap(array, "fsdp", (1, 1))


def doubled(masks):
    order = [0]
    for mask in masks:
        order = order + [o ^ mask for o in order]
    return order


def table(core, orders):
    first, second = (jnp.array(order, dtype=jnp.int32) for order in orders)
    return jnp.where(core == 0, first, second)


def by_core(core, own, other, axis):
    return jnp.where(
        core == 0,
        jnp.concatenate([own, other], axis=axis),
        jnp.concatenate([other, own], axis=axis),
    )


def call(kernel, outs, args, flops=0, vmem=8, scratch=(), smem=0, after=()):
    moved = sum(a.size * a.dtype.itemsize for a in args)
    moved += sum(o.size * o.dtype.itemsize for o in outs)
    specs = [
        pl.BlockSpec(memory_space=pltpu.SMEM if i < smem else pltpu.VMEM)
        for i in range(len(args))
    ]
    count = len(args)

    def body(*refs):
        kernel(*refs[:count], *refs[count + len(after) :])

    specs += [pl.BlockSpec(memory_space=pl.ANY) for _ in after]
    return pl.pallas_call(
        body,
        out_shape=list(outs),
        in_specs=specs,
        out_specs=[pl.BlockSpec(memory_space=pltpu.VMEM) for _ in outs],
        scratch_shapes=list(scratch),
        compiler_params=pltpu.CompilerParams(vmem_limit_bytes=vmem * MIB),
        cost_estimate=pl.CostEstimate(flops=flops, bytes_accessed=moved, transcendentals=0),
    )(*args, *after)


def shape(rows, columns, kind):
    return jax.ShapeDtypeStruct((rows, columns), kind)


def with_mark(kernel):
    def body(*refs):
        refs[-1][...] = jnp.zeros(refs[-1].shape, refs[-1].dtype)
        kernel(*refs[:-1])

    return body


def stack_kernel(sizes, *refs):
    outs = refs[sum(sizes) :]
    at = 0
    for size, out_ref in zip(sizes, outs):
        row = 0
        for ref in refs[at : at + size]:
            out_ref[row : row + ref.shape[0], :] = ref[...]
            row += ref.shape[0]
        at += size


def stack(groups):
    outs = [shape(sum(a.shape[0] for a in g), g[0].shape[1], g[0].dtype) for g in groups]
    return call(
        functools.partial(stack_kernel, [len(g) for g in groups]),
        outs,
        [a for g in groups for a in g],
    )


def stack_marked(groups, after):
    outs = [shape(sum(a.shape[0] for a in g), g[0].shape[1], g[0].dtype) for g in groups]
    *result, mark = call(
        with_mark(functools.partial(stack_kernel, [len(g) for g in groups])),
        [*outs, shape(8, 128, F32)],
        [a for g in groups for a in g],
        after=after,
    )
    return result, mark


def reorder_kernel(width, index_ref, in_ref, out_ref):
    for k in range(out_ref.shape[1] // width):
        start = pl.multiple_of(index_ref[k] * width, width)
        out_ref[:, k * width : (k + 1) * width] = in_ref[:, pl.ds(start, width)]


def reorder(array, index, width):
    outs = [shape(array.shape[0], array.shape[1], array.dtype)]
    return call(
        functools.partial(reorder_kernel, width), outs, [index, array], vmem=8, smem=1
    )[0]


def sums_kernel(count, block, index_ref, own_ref, other_ref, grads_ref, *refs):
    outs, chosen = refs[:count], refs[count]
    tokens = own_ref.shape[1]
    at = 0
    for part, out_ref in enumerate(outs):
        blocks = out_ref.shape[0] // block
        for k in range(blocks):
            row = slice(k * block, (k + 1) * block)
            start = pl.multiple_of(index_ref[part * blocks + k] * block, block)
            chosen[row, :tokens] = own_ref[pl.ds(start, block), :]
            chosen[row, tokens:] = other_ref[pl.ds(start, block), :]
        width = out_ref.shape[1]
        out_ref[...] = jnp.dot(
            chosen[...], grads_ref[:, at : at + width], preferred_element_type=F32
        ).astype(out_ref.dtype)
        at += width


def partial_sums(index, own, other, grads, rows, widths, block, kind, after=()):
    return call(
        functools.partial(sums_kernel, len(widths), block),
        [shape(rows, w, kind) for w in widths],
        [index, own, other, grads],
        flops=2 * rows * grads.size,
        vmem=8,
        scratch=[pltpu.VMEM((rows, 2 * own.shape[1]), BF)],
        smem=1,
        after=after,
    )


def halve_kernel(count, *refs):
    kept, got, kept_out, sent = (refs[i * count : (i + 1) * count] for i in range(4))
    for k, g, o, s in zip(kept, got, kept_out, sent):
        rows = o.shape[0]
        s[...] = (k[rows:, :] + g[rows:, :].astype(F32)).astype(s.dtype)
        o[...] = k[:rows, :] + g[:rows, :].astype(F32)


def halve(kept, got, after):
    rows = kept[0].shape[0] // 2
    outs = [shape(rows, k.shape[1], kind) for kind in (F32, BF) for k in kept]
    *result, mark = call(
        with_mark(functools.partial(halve_kernel, len(kept))),
        [*outs, shape(8, 128, F32)],
        [*kept, *got],
        after=after,
    )
    return result[: len(kept)], result[len(kept) :], mark


def adam_kernel(count, *refs):
    kept, got = refs[:count], refs[count : 2 * count]
    first_ref, second_ref = refs[2 * count : 2 * count + 2]
    new_first_ref, new_second_ref = refs[2 * count + 2 : 2 * count + 4]
    directions = refs[2 * count + 4 :]
    at = 0
    for k, g, d in zip(kept, got, directions):
        span = slice(at, at + k.shape[1])
        at += k.shape[1]
        lowrank = k[...] + g[...].astype(F32)
        new_first = 0.9 * first_ref[:, span] + 0.1 * lowrank
        new_second = 0.99 * second_ref[:, span] + 0.01 * lowrank * lowrank
        new_first_ref[:, span] = new_first
        new_second_ref[:, span] = new_second
        d[...] = (new_first / first_fix / (jnp.sqrt(new_second / second_fix) + 1e-08)).astype(
            d.dtype
        )


def adam(kept, got, first, second, after):
    outs = [shape(*first.shape, F32)] * 2 + [shape(*k.shape, BF) for k in kept]
    result = call(
        functools.partial(adam_kernel, len(kept)),
        outs,
        [*kept, *got, first, second],
        after=after,
    )
    return result[0], result[1], result[2:]


def pick_kernel(which_ref, first_ref, second_ref, out_ref):
    rows = out_ref.shape[0] // 2
    start = pl.multiple_of(which_ref[0] * rows, rows)
    out_ref[:rows, :] = first_ref[pl.ds(start, rows), :]
    out_ref[rows:, :] = second_ref[pl.ds(start, rows), :]


def join_kernel(core_ref, first_ref, second_ref, other_ref, out_first_ref, out_second_ref):
    rows, half = out_first_ref.shape[0], first_ref.shape[1]
    core = core_ref[0]
    start = pl.multiple_of(core * rows, rows)
    own = pl.ds(pl.multiple_of(core * half, half), half)
    other = pl.ds(pl.multiple_of((1 - core) * half, half), half)
    out_first_ref[:, own] = first_ref[pl.ds(start, rows), :]
    out_first_ref[:, other] = other_ref[:rows, :]
    out_second_ref[:, own] = second_ref[pl.ds(start, rows), :]
    out_second_ref[:, other] = other_ref[rows:, :]


def early_kernel(count, *refs):
    factors, parts, out_ref = refs[:count], refs[count : 2 * count], refs[2 * count]
    at = 0
    for f, p in zip(factors, parts):
        depth, width = p.shape
        out_ref[:, at : at + width] = jnp.dot(
            f[:, :depth], p[...], preferred_element_type=F32
        )
        at += width


def late_kernel(count, row, at, *refs):
    factors, parts, sum_ref, out_ref = (
        refs[:count],
        refs[count : 2 * count],
        refs[2 * count],
        refs[2 * count + 1],
    )
    rows = out_ref.shape[0]
    to = 0
    for f, p in zip(factors, parts):
        depth, width = p.shape
        product = jnp.dot(f[row : row + rows, depth:], p[...], preferred_element_type=F32)
        out_ref[:, to : to + width] = (
            sum_ref[row : row + rows, at : at + width] + product
        ).astype(out_ref.dtype)
        at += width
        to += width


def body(activations, grad_output, projector, first_moment, second_moment):
    place = lax.axis_index("fsdp").astype(jnp.int32)
    tp_place = lax.axis_index("tp").astype(jnp.int32)
    core = place & 1
    chip = place >> 1
    tokens, width = grad_output.shape
    half = width // 2
    rank = projector.shape[1]
    block = rank // 16
    column_count = rank // 8
    wide = half * 5 // 7
    widths = (wide, half - wide)
    rows = first_moment.shape[0]

    def my_half(array):
        return lax.dynamic_slice_in_dim(array, core * half, half, 1)

    def other_half(array):
        return lax.dynamic_slice_in_dim(array, (1 - core) * half, half, 1)

    columns = lax.dynamic_slice_in_dim(projector, tp_place * column_count, column_count, 1)
    for masks in ((8, 16, 24), (2, 4, 6)):
        columns = stack([[columns] + [swap(columns, "fsdp", (m, m)) for m in masks]])[0]
    columns_other = swap_core(columns)
    order = jnp.array([x + z for x in (0, 2, 4, 6) for z in (0, 8, 16, 24)], jnp.int32)
    index = jnp.concatenate([place ^ order, place ^ 1 ^ order])
    act = reorder(activations, index, projector.shape[0])
    depth = columns.shape[0]
    dims = (((0,), (1,)), ((), ()))
    own = lax.dot_general(columns, act[:, :depth], dims, preferred_element_type=F32)
    own = own + lax.dot_general(columns_other, act[:, depth:], dims, preferred_element_type=F32)
    own = own.astype(BF)

    coords = stack([[own, swap(own, "tp", (1, 1))]])[0]
    coords = stack([[coords] + [swap(coords, "tp", (m, m)) for m in (2, 4, 6)]])[0]
    coords_other = swap_core(coords)

    grads = jnp.concatenate(
        [my_half(grad_output), swap_core(other_half(grad_output))], axis=0
    )
    moments = jnp.concatenate([first_moment, second_moment], axis=0)
    moments_other = swap_core(other_half(moments))
    moments_own = my_half(moments)
    first = by_core(core, moments_own[:rows], moments_other[:rows], 0)
    second = by_core(core, moments_own[rows:], moments_other[rows:], 0)
    both = jnp.concatenate([projector, swap_core(projector)], axis=0)

    sum_orders = (([1, 3, 4, 12], [3, 1, 12, 4]), ([4, 12, 1, 3], [12, 4, 3, 1]))
    back_orders = [[o[::-1] for o in orders] for orders in sum_orders]
    keep_index, send_index = [], []
    for orders in sum_orders:
        wanted = chip ^ table(core, [doubled(o[::-1]) for o in orders])
        position = 2 * (tp_place ^ (wanted >> 1)) + (wanted & 1)
        keep_index.append(position[:8])
        send_index.append(position[8:])
    ranks = jnp.arange(rank, dtype=jnp.int32)
    factors = []
    for orders in back_orders:
        blocks = chip ^ table(core, [doubled(o) for o in orders])
        wanted = (blocks[:, None] * block + ranks[None, :block]).reshape(-1)
        choose = (ranks[:, None] == wanted[None, :]).astype(BF)
        factors.append(jnp.dot(both, choose, preferred_element_type=F32).astype(BF))

    def exchange(arrays, orders_of, stage):
        return [
            swap(a, "fsdp", [2 * o[stage] for o in orders]) for a, orders in zip(arrays, orders_of)
        ]

    arrays = (coords, coords_other, grads, rank // 2, widths, block)
    sent = partial_sums(jnp.concatenate(send_index), *arrays, BF)
    kept = partial_sums(jnp.concatenate(keep_index), *arrays, F32)
    marks = []
    for stage in range(3):
        kept, sent, mark = halve(kept, exchange(sent, sum_orders, stage), marks)
        marks = [swap_core(mark)]
    got = exchange(sent, sum_orders, 3)
    new_first, new_second, parts = adam(kept, got, first, second, [*factors, *marks])

    states_other = swap_core(
        call(
            pick_kernel,
            [shape(2 * rows, half, F32)],
            [(1 - core)[None], new_first, new_second],
            smem=1,
        )[0]
    )
    out_first, out_second, joined = call(
        with_mark(join_kernel),
        [shape(rows, width, F32)] * 2 + [shape(8, 128, F32)],
        [core[None], new_first, new_second, states_other],
        smem=1,
    )
    marks = [states_other]
    for stage in range(4):
        got = exchange(parts, back_orders, stage)
        if stage == 1:
            marks = [*marks, joined]
        if stage < 3:
            parts, mark = stack_marked([[p, g] for p, g in zip(parts, got)], marks)
            marks = [swap_core(mark)]
    count = len(parts)
    flops = rank * half * both.shape[0]
    early = call(
        functools.partial(early_kernel, count),
        [shape(both.shape[0], half, F32)],
        [*factors, *parts],
        flops=flops,
        vmem=8,
        after=marks,
    )[0]

    def late(row, parts, after=()):
        at = sum(widths[: parts.start])
        span = sum(widths[parts])
        return call(
            functools.partial(late_kernel, len(widths[parts]), row, at),
            [shape(tokens, span, BF)],
            [*factors[parts], *got[parts], early],
            flops=rank * tokens * span,
            after=after,
        )[0]

    every = slice(0, count)
    other = swap_core(late(tokens, every))
    update = by_core(core, late(0, every), other, 1)
    return (out_first, out_second, update)


def solution(mesh):
    return jax.shard_map(
        body,
        mesh=mesh,
        in_specs=(
            P("fsdp", None),
            P("fsdp", "tp"),
            P("fsdp", None),
            P("fsdp", "tp"),
            P("fsdp", "tp"),
        ),
        out_specs=(P("fsdp", "tp"), P("fsdp", "tp"), P("fsdp", "tp")),
        check_vma=False,
    )
```

```python
import functools

import jax
import jax.numpy as jnp
from jax import lax
from jax.experimental import pallas as pl
from jax.experimental.pallas import tpu as pltpu
from jax.sharding import PartitionSpec as P

first_fix = 0.9999734386011124
second_fix = 0.6339676587267705
BF = jnp.bfloat16
F32 = jnp.float32
MIB = 2**20


def swap(array, axis, masks):
    inner = lax.axis_size("tp")
    count = lax.axis_size("fsdp") * inner
    scale = inner if axis == "fsdp" else 1
    return lax.ppermute(
        array, ("fsdp", "tp"), [(i, i ^ (scale * masks[i // inner % 2])) for i in range(count)]
    )


def swap_core(array):
    return swap(array, "fsdp", (1, 1))


def doubled(masks):
    order = [0]
    for mask in masks:
        order = order + [o ^ mask for o in order]
    return order


def table(core, orders):
    first, second = (jnp.array(order, dtype=jnp.int32) for order in orders)
    return jnp.where(core == 0, first, second)


def by_core(core, own, other, axis):
    return jnp.where(
        core == 0,
        jnp.concatenate([own, other], axis=axis),
        jnp.concatenate([other, own], axis=axis),
    )


def call(kernel, outs, args, flops=0, vmem=8, scratch=(), smem=0, after=()):
    moved = sum(a.size * a.dtype.itemsize for a in args)
    moved += sum(o.size * o.dtype.itemsize for o in outs)
    specs = [
        pl.BlockSpec(memory_space=pltpu.SMEM if i < smem else pltpu.VMEM)
        for i in range(len(args))
    ]
    count = len(args)

    def body(*refs):
        kernel(*refs[:count], *refs[count + len(after) :])

    specs += [pl.BlockSpec(memory_space=pl.ANY) for _ in after]
    return pl.pallas_call(
        body,
        out_shape=list(outs),
        in_specs=specs,
        out_specs=[pl.BlockSpec(memory_space=pltpu.VMEM) for _ in outs],
        scratch_shapes=list(scratch),
        compiler_params=pltpu.CompilerParams(vmem_limit_bytes=vmem * MIB),
        cost_estimate=pl.CostEstimate(flops=flops, bytes_accessed=moved, transcendentals=0),
    )(*args, *after)


def shape(rows, columns, kind):
    return jax.ShapeDtypeStruct((rows, columns), kind)


def with_mark(kernel):
    def body(*refs):
        refs[-1][...] = jnp.zeros(refs[-1].shape, refs[-1].dtype)
        kernel(*refs[:-1])

    return body


def stack_kernel(sizes, *refs):
    outs = refs[sum(sizes) :]
    at = 0
    for size, out_ref in zip(sizes, outs):
        row = 0
        for ref in refs[at : at + size]:
            out_ref[row : row + ref.shape[0], :] = ref[...]
            row += ref.shape[0]
        at += size


def stack(groups, after=()):
    outs = [shape(sum(a.shape[0] for a in g), g[0].shape[1], g[0].dtype) for g in groups]
    return call(
        functools.partial(stack_kernel, [len(g) for g in groups]),
        outs,
        [a for g in groups for a in g],
        after=after,
    )


def stack_marked(groups, after):
    outs = [shape(sum(a.shape[0] for a in g), g[0].shape[1], g[0].dtype) for g in groups]
    *result, mark = call(
        with_mark(functools.partial(stack_kernel, [len(g) for g in groups])),
        [*outs, shape(8, 128, F32)],
        [a for g in groups for a in g],
        after=after,
    )
    return result, mark


def reorder_kernel(width, index_ref, in_ref, out_ref):
    for k in range(out_ref.shape[1] // width):
        start = pl.multiple_of(index_ref[k] * width, width)
        out_ref[:, k * width : (k + 1) * width] = in_ref[:, pl.ds(start, width)]


def reorder(array, index, width, after):
    outs = [shape(array.shape[0], array.shape[1], array.dtype)]
    return call(
        functools.partial(reorder_kernel, width), outs, [index, array], smem=1, after=after
    )[0]


def sums_kernel(count, block, index_ref, own_ref, other_ref, grads_ref, *refs):
    outs, chosen = refs[:count], refs[count]
    tokens = own_ref.shape[1]
    at = 0
    for part, out_ref in enumerate(outs):
        blocks = out_ref.shape[0] // block
        for k in range(blocks):
            row = slice(k * block, (k + 1) * block)
            start = pl.multiple_of(index_ref[part * blocks + k] * block, block)
            chosen[row, :tokens] = own_ref[pl.ds(start, block), :]
            chosen[row, tokens:] = other_ref[pl.ds(start, block), :]
        width = out_ref.shape[1]
        out_ref[...] = jnp.dot(
            chosen[...], grads_ref[:, at : at + width], preferred_element_type=F32
        ).astype(out_ref.dtype)
        at += width


def partial_sums(index, own, other, grads, rows, widths, block, kind, after=()):
    return call(
        functools.partial(sums_kernel, len(widths), block),
        [shape(rows, w, kind) for w in widths],
        [index, own, other, grads],
        flops=2 * rows * grads.size,
        vmem=8,
        scratch=[pltpu.VMEM((rows, 2 * own.shape[1]), BF)],
        smem=1,
        after=after,
    )


def halve_kernel(count, *refs):
    kept, got, kept_out, sent = (refs[i * count : (i + 1) * count] for i in range(4))
    for k, g, o, s in zip(kept, got, kept_out, sent):
        rows = o.shape[0]
        s[...] = (k[rows:, :] + g[rows:, :].astype(F32)).astype(s.dtype)
        o[...] = k[:rows, :] + g[:rows, :].astype(F32)


def halve(kept, got, after):
    rows = kept[0].shape[0] // 2
    outs = [shape(rows, k.shape[1], kind) for kind in (F32, BF) for k in kept]
    *result, mark = call(
        with_mark(functools.partial(halve_kernel, len(kept))),
        [*outs, shape(8, 128, F32)],
        [*kept, *got],
        after=after,
    )
    return result[: len(kept)], result[len(kept) :], mark


def adam_kernel(count, *refs):
    kept, got = refs[:count], refs[count : 2 * count]
    first_ref, second_ref = refs[2 * count : 2 * count + 2]
    new_first_ref, new_second_ref = refs[2 * count + 2 : 2 * count + 4]
    directions = refs[2 * count + 4 :]
    at = 0
    for k, g, d in zip(kept, got, directions):
        span = slice(at, at + k.shape[1])
        at += k.shape[1]
        lowrank = k[...] + g[...].astype(F32)
        new_first = 0.9 * first_ref[:, span] + 0.1 * lowrank
        new_second = 0.99 * second_ref[:, span] + 0.01 * lowrank * lowrank
        new_first_ref[:, span] = new_first
        new_second_ref[:, span] = new_second
        d[...] = (new_first / first_fix / (jnp.sqrt(new_second / second_fix) + 1e-08)).astype(
            d.dtype
        )


def adam(kept, got, first, second, after):
    outs = [shape(*first.shape, F32)] * 2 + [shape(*k.shape, BF) for k in kept]
    result = call(
        functools.partial(adam_kernel, len(kept)),
        outs,
        [*kept, *got, first, second],
        after=after,
    )
    return result[0], result[1], result[2:]


def split_kernel(core_ref, first_ref, second_ref, own_ref, other_ref):
    rows, half = first_ref.shape[0], own_ref.shape[1]
    core = core_ref[0]
    own = pl.ds(pl.multiple_of(core * half, half), half)
    other = pl.ds(pl.multiple_of((1 - core) * half, half), half)
    own_ref[:rows, :] = first_ref[:, own]
    own_ref[rows:, :] = second_ref[:, own]
    other_ref[:rows, :] = first_ref[:, other]
    other_ref[rows:, :] = second_ref[:, other]


def merge_kernel(core_ref, own_ref, got_ref, first_ref, second_ref):
    rows = own_ref.shape[0] // 2
    core = core_ref[0]
    own = pl.ds(pl.multiple_of(core * rows, rows), rows)
    other = pl.ds(pl.multiple_of((1 - core) * rows, rows), rows)
    first_ref[own, :] = own_ref[:rows, :]
    first_ref[other, :] = got_ref[:rows, :]
    second_ref[own, :] = own_ref[rows:, :]
    second_ref[other, :] = got_ref[rows:, :]


def pick_kernel(which_ref, first_ref, second_ref, out_ref):
    rows = out_ref.shape[0] // 2
    start = pl.multiple_of(which_ref[0] * rows, rows)
    out_ref[:rows, :] = first_ref[pl.ds(start, rows), :]
    out_ref[rows:, :] = second_ref[pl.ds(start, rows), :]


def join_kernel(core_ref, first_ref, second_ref, other_ref, out_first_ref, out_second_ref):
    rows, half = out_first_ref.shape[0], first_ref.shape[1]
    core = core_ref[0]
    start = pl.multiple_of(core * rows, rows)
    own = pl.ds(pl.multiple_of(core * half, half), half)
    other = pl.ds(pl.multiple_of((1 - core) * half, half), half)
    out_first_ref[:, own] = first_ref[pl.ds(start, rows), :]
    out_first_ref[:, other] = other_ref[:rows, :]
    out_second_ref[:, own] = second_ref[pl.ds(start, rows), :]
    out_second_ref[:, other] = other_ref[rows:, :]


def early_kernel(count, *refs):
    factors, parts, out_ref = refs[:count], refs[count : 2 * count], refs[2 * count]
    at = 0
    for f, p in zip(factors, parts):
        depth, width = p.shape
        out_ref[:, at : at + width] = jnp.dot(
            f[:, :depth], p[...], preferred_element_type=F32
        )
        at += width


def late_kernel(count, row, at, *refs):
    factors, parts, sum_ref, out_ref = (
        refs[:count],
        refs[count : 2 * count],
        refs[2 * count],
        refs[2 * count + 1],
    )
    rows = out_ref.shape[0]
    to = 0
    for f, p in zip(factors, parts):
        depth, width = p.shape
        product = jnp.dot(f[row : row + rows, depth:], p[...], preferred_element_type=F32)
        out_ref[:, to : to + width] = (
            sum_ref[row : row + rows, at : at + width] + product
        ).astype(out_ref.dtype)
        at += width
        to += width


def body(activations, grad_output, projector, first_moment, second_moment):
    place = lax.axis_index("fsdp").astype(jnp.int32)
    tp_place = lax.axis_index("tp").astype(jnp.int32)
    core = place & 1
    chip = place >> 1
    tokens, width = grad_output.shape
    half = width // 2
    rank = projector.shape[1]
    block = rank // 16
    column_count = rank // 8
    wide = half * 5 // 7
    widths = (wide, half - wide)
    rows = first_moment.shape[0]

    def my_half(array):
        return lax.dynamic_slice_in_dim(array, core * half, half, 1)

    def other_half(array):
        return lax.dynamic_slice_in_dim(array, (1 - core) * half, half, 1)

    sum_orders = (([1, 3, 4, 12], [3, 1, 12, 4]), ([4, 12, 1, 3], [12, 4, 3, 1]))
    back_orders = [[o[::-1] for o in orders] for orders in sum_orders]
    ranks = jnp.arange(rank, dtype=jnp.int32)
    rank_tables = []
    for orders in back_orders:
        blocks = chip ^ table(core, [doubled(o) for o in orders])
        rank_tables.append((blocks[:, None] * block + ranks[None, :block]).reshape(-1))

    moments_own, moments_other = call(
        split_kernel,
        [shape(2 * rows, half, F32)] * 2,
        [core[None], first_moment, second_moment],
        smem=1,
    )
    moments_got = swap_core(moments_other)
    projector_other = swap_core(projector)

    grads_got = swap_core(other_half(grad_output))
    order = jnp.array([x + z for x in (0, 2, 4, 6) for z in (0, 8, 16, 24)], jnp.int32)
    index = jnp.concatenate([place ^ order, place ^ 1 ^ order])
    act = reorder(activations, index, projector.shape[0], rank_tables)

    columns = lax.dynamic_slice_in_dim(projector, tp_place * column_count, column_count, 1)
    for masks, after in (((8, 16, 24), ()), ((2, 4, 6), (act, grads_got))):
        got = [swap(columns, "fsdp", (m, m)) for m in masks]
        columns = stack([[columns] + got], after)[0]
    columns_other = swap_core(columns)
    depth = columns.shape[0]
    dims = (((0,), (1,)), ((), ()))
    own = lax.dot_general(columns, act[:, :depth], dims, preferred_element_type=F32)
    own = own + lax.dot_general(columns_other, act[:, depth:], dims, preferred_element_type=F32)
    own = own.astype(BF)

    coords = stack([[own, swap(own, "tp", (1, 1))]])[0]
    coords = stack(
        [[coords] + [swap(coords, "tp", (m, m)) for m in (2, 4, 6)]],
        [moments_got, projector_other],
    )[0]
    coords_other = swap_core(coords)

    grads = jnp.concatenate(
        [my_half(grad_output), grads_got], axis=0
    )
    first, second = call(
        merge_kernel,
        [shape(2 * rows, half, F32)] * 2,
        [core[None], moments_own, moments_got],
        smem=1,
    )
    both = jnp.concatenate([projector, projector_other], axis=0)

    keep_index, send_index = [], []
    for orders in sum_orders:
        wanted = chip ^ table(core, [doubled(o[::-1]) for o in orders])
        position = 2 * (tp_place ^ (wanted >> 1)) + (wanted & 1)
        keep_index.append(position[:8])
        send_index.append(position[8:])
    factors = []
    for wanted in rank_tables:
        choose = (ranks[:, None] == wanted[None, :]).astype(BF)
        factors.append(jnp.dot(both, choose, preferred_element_type=F32).astype(BF))

    def exchange(arrays, orders_of, stage):
        return [
            swap(a, "fsdp", [2 * o[stage] for o in orders]) for a, orders in zip(arrays, orders_of)
        ]

    arrays = (coords, coords_other, grads, rank // 2, widths, block)
    sent = partial_sums(jnp.concatenate(send_index), *arrays, BF)
    kept = partial_sums(jnp.concatenate(keep_index), *arrays, F32)
    marks = []
    for stage in range(3):
        kept, sent, mark = halve(kept, exchange(sent, sum_orders, stage), marks)
        marks = [swap_core(mark)]
    got = exchange(sent, sum_orders, 3)
    new_first, new_second, parts = adam(kept, got, first, second, [*factors, *marks])

    states_other = swap_core(
        call(
            pick_kernel,
            [shape(2 * rows, half, F32)],
            [(1 - core)[None], new_first, new_second],
            smem=1,
        )[0]
    )
    out_first, out_second, joined = call(
        with_mark(join_kernel),
        [shape(rows, width, F32)] * 2 + [shape(8, 128, F32)],
        [core[None], new_first, new_second, states_other],
        smem=1,
    )
    marks = [states_other]
    for stage in range(4):
        got = exchange(parts, back_orders, stage)
        if stage == 1:
            marks = [*marks, joined]
        if stage < 3:
            parts, mark = stack_marked([[p, g] for p, g in zip(parts, got)], marks)
            marks = [swap_core(mark)]
    count = len(parts)
    flops = rank * half * both.shape[0]
    early = call(
        functools.partial(early_kernel, count),
        [shape(both.shape[0], half, F32)],
        [*factors, *parts],
        flops=flops,
        vmem=8,
        after=marks,
    )[0]

    def late(row, parts, after=()):
        at = sum(widths[: parts.start])
        span = sum(widths[parts])
        return call(
            functools.partial(late_kernel, len(widths[parts]), row, at),
            [shape(tokens, span, BF)],
            [*factors[parts], *got[parts], early],
            flops=rank * tokens * span,
            after=after,
        )[0]

    every = slice(0, count)
    other = swap_core(late(tokens, every))
    update = by_core(core, late(0, every), other, 1)
    return (out_first, out_second, update)


def solution(mesh):
    return jax.shard_map(
        body,
        mesh=mesh,
        in_specs=(
            P("fsdp", None),
            P("fsdp", "tp"),
            P("fsdp", None),
            P("fsdp", "tp"),
            P("fsdp", "tp"),
        ),
        out_specs=(P("fsdp", "tp"), P("fsdp", "tp"), P("fsdp", "tp")),
        check_vma=False,
    )
```

```python
import functools

import jax
import jax.numpy as jnp
from jax import lax
from jax.experimental import pallas as pl
from jax.experimental.pallas import tpu as pltpu
from jax.sharding import PartitionSpec as P

first_fix = 0.9999734386011124
second_fix = 0.6339676587267705
BF = jnp.bfloat16
F32 = jnp.float32
MIB = 2**20


def swap(array, axis, masks):
    inner = lax.axis_size("tp")
    count = lax.axis_size("fsdp") * inner
    scale = inner if axis == "fsdp" else 1
    return lax.ppermute(
        array, ("fsdp", "tp"), [(i, i ^ (scale * masks[i // inner % 2])) for i in range(count)]
    )


def swap_core(array):
    return swap(array, "fsdp", (1, 1))


def doubled(masks):
    order = [0]
    for mask in masks:
        order = order + [o ^ mask for o in order]
    return order


def table(core, orders):
    first, second = (jnp.array(order, dtype=jnp.int32) for order in orders)
    return jnp.where(core == 0, first, second)


def by_core(core, own, other, axis):
    return jnp.where(
        core == 0,
        jnp.concatenate([own, other], axis=axis),
        jnp.concatenate([other, own], axis=axis),
    )


def call(kernel, outs, args, flops=0, vmem=8, scratch=(), smem=0, after=()):
    moved = sum(a.size * a.dtype.itemsize for a in args)
    moved += sum(o.size * o.dtype.itemsize for o in outs)
    specs = [
        pl.BlockSpec(memory_space=pltpu.SMEM if i < smem else pltpu.VMEM)
        for i in range(len(args))
    ]
    count = len(args)

    def body(*refs):
        kernel(*refs[:count], *refs[count + len(after) :])

    specs += [pl.BlockSpec(memory_space=pl.ANY) for _ in after]
    return pl.pallas_call(
        body,
        out_shape=list(outs),
        in_specs=specs,
        out_specs=[pl.BlockSpec(memory_space=pltpu.VMEM) for _ in outs],
        scratch_shapes=list(scratch),
        compiler_params=pltpu.CompilerParams(vmem_limit_bytes=vmem * MIB),
        cost_estimate=pl.CostEstimate(flops=flops, bytes_accessed=moved, transcendentals=0),
    )(*args, *after)


def shape(rows, columns, kind):
    return jax.ShapeDtypeStruct((rows, columns), kind)


def with_mark(kernel):
    def body(*refs):
        refs[-1][...] = jnp.zeros(refs[-1].shape, refs[-1].dtype)
        kernel(*refs[:-1])

    return body


def stack_kernel(sizes, *refs):
    outs = refs[sum(sizes) :]
    at = 0
    for size, out_ref in zip(sizes, outs):
        row = 0
        for ref in refs[at : at + size]:
            out_ref[row : row + ref.shape[0], :] = ref[...]
            row += ref.shape[0]
        at += size


def stack(groups, after=()):
    outs = [shape(sum(a.shape[0] for a in g), g[0].shape[1], g[0].dtype) for g in groups]
    return call(
        functools.partial(stack_kernel, [len(g) for g in groups]),
        outs,
        [a for g in groups for a in g],
        after=after,
    )


def stack_marked(groups, after):
    outs = [shape(sum(a.shape[0] for a in g), g[0].shape[1], g[0].dtype) for g in groups]
    *result, mark = call(
        with_mark(functools.partial(stack_kernel, [len(g) for g in groups])),
        [*outs, shape(8, 128, F32)],
        [a for g in groups for a in g],
        after=after,
    )
    return result, mark


def reorder_kernel(width, index_ref, in_ref, out_ref):
    for k in range(out_ref.shape[1] // width):
        start = pl.multiple_of(index_ref[k] * width, width)
        out_ref[:, k * width : (k + 1) * width] = in_ref[:, pl.ds(start, width)]


def reorder(array, index, width, after):
    outs = [shape(array.shape[0], array.shape[1], array.dtype)]
    return call(
        functools.partial(reorder_kernel, width), outs, [index, array], smem=1, after=after
    )[0]


def sums_kernel(count, block, index_ref, own_ref, other_ref, grads_ref, *refs):
    outs, chosen = refs[:count], refs[count]
    tokens = own_ref.shape[1]
    at = 0
    for part, out_ref in enumerate(outs):
        blocks = out_ref.shape[0] // block
        for k in range(blocks):
            row = slice(k * block, (k + 1) * block)
            start = pl.multiple_of(index_ref[part * blocks + k] * block, block)
            chosen[row, :tokens] = own_ref[pl.ds(start, block), :]
            chosen[row, tokens:] = other_ref[pl.ds(start, block), :]
        width = out_ref.shape[1]
        out_ref[...] = jnp.dot(
            chosen[...], grads_ref[:, at : at + width], preferred_element_type=F32
        ).astype(out_ref.dtype)
        at += width


def partial_sums(index, own, other, grads, rows, widths, block, kind, after=()):
    return call(
        functools.partial(sums_kernel, len(widths), block),
        [shape(rows, w, kind) for w in widths],
        [index, own, other, grads],
        flops=2 * rows * grads.size,
        vmem=8,
        scratch=[pltpu.VMEM((rows, 2 * own.shape[1]), BF)],
        smem=1,
        after=after,
    )


def halve_kernel(count, *refs):
    kept, got, kept_out, sent = (refs[i * count : (i + 1) * count] for i in range(4))
    for k, g, o, s in zip(kept, got, kept_out, sent):
        rows = o.shape[0]
        s[...] = (k[rows:, :] + g[rows:, :].astype(F32)).astype(s.dtype)
        o[...] = k[:rows, :] + g[:rows, :].astype(F32)


def halve(kept, got, after):
    rows = kept[0].shape[0] // 2
    outs = [shape(rows, k.shape[1], kind) for kind in (F32, BF) for k in kept]
    *result, mark = call(
        with_mark(functools.partial(halve_kernel, len(kept))),
        [*outs, shape(8, 128, F32)],
        [*kept, *got],
        after=after,
    )
    return result[: len(kept)], result[len(kept) :], mark


def adam_kernel(count, *refs):
    core_ref, kept, got = refs[0], refs[1 : 1 + count], refs[1 + count : 1 + 2 * count]
    first_ref, second_ref, new_first_ref, new_second_ref, other_ref = refs[
        1 + 2 * count : 6 + 2 * count
    ]
    directions = refs[6 + 2 * count :]
    at = 0
    for k, g, d in zip(kept, got, directions):
        span = slice(at, at + k.shape[1])
        at += k.shape[1]
        lowrank = k[...] + g[...].astype(F32)
        new_first = 0.9 * first_ref[:, span] + 0.1 * lowrank
        new_second = 0.99 * second_ref[:, span] + 0.01 * lowrank * lowrank
        new_first_ref[:, span] = new_first
        new_second_ref[:, span] = new_second
        d[...] = (new_first / first_fix / (jnp.sqrt(new_second / second_fix) + 1e-08)).astype(
            d.dtype
        )
    rows = other_ref.shape[0] // 2
    start = pl.multiple_of((1 - core_ref[0]) * rows, rows)
    other_ref[:rows, :] = new_first_ref[pl.ds(start, rows), :]
    other_ref[rows:, :] = new_second_ref[pl.ds(start, rows), :]


def adam(core, kept, got, first, second, after):
    outs = [shape(*first.shape, F32)] * 3 + [shape(*k.shape, BF) for k in kept]
    result = call(
        functools.partial(adam_kernel, len(kept)),
        outs,
        [core[None], *kept, *got, first, second],
        smem=1,
        after=after,
    )
    return *result[:3], result[3:]


def split_kernel(core_ref, first_ref, second_ref, own_ref, other_ref):
    rows, half = first_ref.shape[0], own_ref.shape[1]
    core = core_ref[0]
    own = pl.ds(pl.multiple_of(core * half, half), half)
    other = pl.ds(pl.multiple_of((1 - core) * half, half), half)
    own_ref[:rows, :] = first_ref[:, own]
    own_ref[rows:, :] = second_ref[:, own]
    other_ref[:rows, :] = first_ref[:, other]
    other_ref[rows:, :] = second_ref[:, other]


def merge_kernel(core_ref, own_ref, got_ref, first_ref, second_ref):
    rows = own_ref.shape[0] // 2
    core = core_ref[0]
    own = pl.ds(pl.multiple_of(core * rows, rows), rows)
    other = pl.ds(pl.multiple_of((1 - core) * rows, rows), rows)
    first_ref[own, :] = own_ref[:rows, :]
    first_ref[other, :] = got_ref[:rows, :]
    second_ref[own, :] = own_ref[rows:, :]
    second_ref[other, :] = got_ref[rows:, :]


def join_kernel(core_ref, first_ref, second_ref, other_ref, out_first_ref, out_second_ref):
    rows, half = out_first_ref.shape[0], first_ref.shape[1]
    core = core_ref[0]
    start = pl.multiple_of(core * rows, rows)
    own = pl.ds(pl.multiple_of(core * half, half), half)
    other = pl.ds(pl.multiple_of((1 - core) * half, half), half)
    out_first_ref[:, own] = first_ref[pl.ds(start, rows), :]
    out_first_ref[:, other] = other_ref[:rows, :]
    out_second_ref[:, own] = second_ref[pl.ds(start, rows), :]
    out_second_ref[:, other] = other_ref[rows:, :]


def early_kernel(count, *refs):
    factors, parts, out_ref = refs[:count], refs[count : 2 * count], refs[2 * count]
    at = 0
    for f, p in zip(factors, parts):
        depth, width = p.shape
        out_ref[:, at : at + width] = jnp.dot(
            f[:, :depth], p[...], preferred_element_type=F32
        )
        at += width


def late_kernel(count, row, at, *refs):
    factors, parts, sum_ref, out_ref = (
        refs[:count],
        refs[count : 2 * count],
        refs[2 * count],
        refs[2 * count + 1],
    )
    rows = out_ref.shape[0]
    to = 0
    for f, p in zip(factors, parts):
        depth, width = p.shape
        product = jnp.dot(f[row : row + rows, depth:], p[...], preferred_element_type=F32)
        out_ref[:, to : to + width] = (
            sum_ref[row : row + rows, at : at + width] + product
        ).astype(out_ref.dtype)
        at += width
        to += width


def body(activations, grad_output, projector, first_moment, second_moment):
    place = lax.axis_index("fsdp").astype(jnp.int32)
    tp_place = lax.axis_index("tp").astype(jnp.int32)
    core = place & 1
    chip = place >> 1
    tokens, width = grad_output.shape
    half = width // 2
    rank = projector.shape[1]
    block = rank // 16
    column_count = rank // 8
    wide = half * 5 // 7
    widths = (wide, half - wide)
    rows = first_moment.shape[0]

    def my_half(array):
        return lax.dynamic_slice_in_dim(array, core * half, half, 1)

    def other_half(array):
        return lax.dynamic_slice_in_dim(array, (1 - core) * half, half, 1)

    sum_orders = (([1, 3, 4, 12], [3, 1, 12, 4]), ([4, 12, 1, 3], [12, 4, 3, 1]))
    back_orders = [[o[::-1] for o in orders] for orders in sum_orders]
    ranks = jnp.arange(rank, dtype=jnp.int32)
    rank_tables = []
    for orders in back_orders:
        blocks = chip ^ table(core, [doubled(o) for o in orders])
        rank_tables.append((blocks[:, None] * block + ranks[None, :block]).reshape(-1))

    moments_own, moments_other = call(
        split_kernel,
        [shape(2 * rows, half, F32)] * 2,
        [core[None], first_moment, second_moment],
        smem=1,
    )
    moments_got = swap_core(moments_other)
    projector_other = swap_core(projector)

    grads_got = swap_core(other_half(grad_output))
    order = jnp.array([x + z for x in (0, 2, 4, 6) for z in (0, 8, 16, 24)], jnp.int32)
    index = jnp.concatenate([place ^ order, place ^ 1 ^ order])
    act = reorder(activations, index, projector.shape[0], rank_tables)

    columns = lax.dynamic_slice_in_dim(projector, tp_place * column_count, column_count, 1)
    for masks, after in (((8, 16, 24), ()), ((2, 4, 6), (act, grads_got))):
        got = [swap(columns, "fsdp", (m, m)) for m in masks]
        columns = stack([[columns] + got], after)[0]
    columns_other = swap_core(columns)
    depth = columns.shape[0]
    dims = (((0,), (1,)), ((), ()))
    own = lax.dot_general(columns, act[:, :depth], dims, preferred_element_type=F32)
    own = own + lax.dot_general(columns_other, act[:, depth:], dims, preferred_element_type=F32)
    own = own.astype(BF)

    coords = stack([[own, swap(own, "tp", (1, 1))]])[0]
    coords = stack(
        [[coords] + [swap(coords, "tp", (m, m)) for m in (2, 4, 6)]],
        [moments_got, projector_other],
    )[0]
    coords_other = swap_core(coords)

    grads = jnp.concatenate(
        [my_half(grad_output), grads_got], axis=0
    )
    first, second = call(
        merge_kernel,
        [shape(2 * rows, half, F32)] * 2,
        [core[None], moments_own, moments_got],
        smem=1,
    )
    both = jnp.concatenate([projector, projector_other], axis=0)

    keep_index, send_index = [], []
    for orders in sum_orders:
        wanted = chip ^ table(core, [doubled(o[::-1]) for o in orders])
        position = 2 * (tp_place ^ (wanted >> 1)) + (wanted & 1)
        keep_index.append(position[:8])
        send_index.append(position[8:])
    factors = []
    for wanted in rank_tables:
        choose = (ranks[:, None] == wanted[None, :]).astype(BF)
        factors.append(jnp.dot(both, choose, preferred_element_type=F32).astype(BF))

    def exchange(arrays, orders_of, stage):
        return [
            swap(a, "fsdp", [2 * o[stage] for o in orders]) for a, orders in zip(arrays, orders_of)
        ]

    arrays = (coords, coords_other, grads, rank // 2, widths, block)
    sent = partial_sums(jnp.concatenate(send_index), *arrays, BF)
    kept = partial_sums(jnp.concatenate(keep_index), *arrays, F32)
    marks = []
    for stage in range(3):
        kept, sent, mark = halve(kept, exchange(sent, sum_orders, stage), marks)
        marks = [swap_core(mark)]
    got = exchange(sent, sum_orders, 3)
    new_first, new_second, states_sent, parts = adam(
        core, kept, got, first, second, [*factors, *marks]
    )

    got = exchange(parts, back_orders, 0)
    states_other = swap_core(states_sent)
    out_first, out_second, joined = call(
        with_mark(join_kernel),
        [shape(rows, width, F32)] * 2 + [shape(8, 128, F32)],
        [core[None], new_first, new_second, states_other],
        smem=1,
    )
    marks = [states_other]
    for stage in range(4):
        if stage > 0:
            got = exchange(parts, back_orders, stage)
        if stage == 1:
            marks = [*marks, joined]
        if stage < 3:
            parts, mark = stack_marked([[p, g] for p, g in zip(parts, got)], marks)
            marks = [swap_core(mark)]
    count = len(parts)
    flops = rank * half * both.shape[0]
    early = call(
        functools.partial(early_kernel, count),
        [shape(both.shape[0], half, F32)],
        [*factors, *parts],
        flops=flops,
        vmem=8,
        after=marks,
    )[0]

    def late(row, parts, after=()):
        at = sum(widths[: parts.start])
        span = sum(widths[parts])
        return call(
            functools.partial(late_kernel, len(widths[parts]), row, at),
            [shape(tokens, span, BF)],
            [*factors[parts], *got[parts], early],
            flops=rank * tokens * span,
            after=after,
        )[0]

    every = slice(0, count)
    other = swap_core(late(tokens, every))
    update = by_core(core, late(0, every), other, 1)
    return (out_first, out_second, update)


def solution(mesh):
    return jax.shard_map(
        body,
        mesh=mesh,
        in_specs=(
            P("fsdp", None),
            P("fsdp", "tp"),
            P("fsdp", None),
            P("fsdp", "tp"),
            P("fsdp", "tp"),
        ),
        out_specs=(P("fsdp", "tp"), P("fsdp", "tp"), P("fsdp", "tp")),
        check_vma=False,
    )
```

```python
import functools

import jax
import jax.numpy as jnp
from jax import lax
from jax.experimental import pallas as pl
from jax.experimental.pallas import tpu as pltpu
from jax.sharding import PartitionSpec as P

first_fix = 0.9999734386011124
second_fix = 0.6339676587267705
BF = jnp.bfloat16
F32 = jnp.float32
MIB = 2**20


def swap(array, axis, masks):
    inner = lax.axis_size("tp")
    count = lax.axis_size("fsdp") * inner
    scale = inner if axis == "fsdp" else 1
    return lax.ppermute(
        array, ("fsdp", "tp"), [(i, i ^ (scale * masks[i // inner % 2])) for i in range(count)]
    )


def swap_core(array):
    return swap(array, "fsdp", (1, 1))


def doubled(masks):
    order = [0]
    for mask in masks:
        order = order + [o ^ mask for o in order]
    return order


def table(core, orders):
    first, second = (jnp.array(order, dtype=jnp.int32) for order in orders)
    return jnp.where(core == 0, first, second)


def by_core(core, own, other, axis):
    return jnp.where(
        core == 0,
        jnp.concatenate([own, other], axis=axis),
        jnp.concatenate([other, own], axis=axis),
    )


def call(kernel, outs, args, flops=0, vmem=8, scratch=(), smem=0, after=()):
    moved = sum(a.size * a.dtype.itemsize for a in args)
    moved += sum(o.size * o.dtype.itemsize for o in outs)
    specs = [
        pl.BlockSpec(memory_space=pltpu.SMEM if i < smem else pltpu.VMEM)
        for i in range(len(args))
    ]
    count = len(args)

    def body(*refs):
        kernel(*refs[:count], *refs[count + len(after) :])

    specs += [pl.BlockSpec(memory_space=pl.ANY) for _ in after]
    return pl.pallas_call(
        body,
        out_shape=list(outs),
        in_specs=specs,
        out_specs=[pl.BlockSpec(memory_space=pltpu.VMEM) for _ in outs],
        scratch_shapes=list(scratch),
        compiler_params=pltpu.CompilerParams(vmem_limit_bytes=vmem * MIB),
        cost_estimate=pl.CostEstimate(flops=flops, bytes_accessed=moved, transcendentals=0),
    )(*args, *after)


def shape(rows, columns, kind):
    return jax.ShapeDtypeStruct((rows, columns), kind)


def with_mark(kernel):
    def body(*refs):
        refs[-1][...] = jnp.zeros(refs[-1].shape, refs[-1].dtype)
        kernel(*refs[:-1])

    return body


def stack_kernel(sizes, *refs):
    outs = refs[sum(sizes) :]
    at = 0
    for size, out_ref in zip(sizes, outs):
        row = 0
        for ref in refs[at : at + size]:
            out_ref[row : row + ref.shape[0], :] = ref[...]
            row += ref.shape[0]
        at += size


def stack(groups, after=()):
    outs = [shape(sum(a.shape[0] for a in g), g[0].shape[1], g[0].dtype) for g in groups]
    return call(
        functools.partial(stack_kernel, [len(g) for g in groups]),
        outs,
        [a for g in groups for a in g],
        after=after,
    )


def stack_marked(groups, after):
    outs = [shape(sum(a.shape[0] for a in g), g[0].shape[1], g[0].dtype) for g in groups]
    *result, mark = call(
        with_mark(functools.partial(stack_kernel, [len(g) for g in groups])),
        [*outs, shape(8, 128, F32)],
        [a for g in groups for a in g],
        after=after,
    )
    return result, mark


def reorder_kernel(width, index_ref, in_ref, out_ref):
    for k in range(out_ref.shape[1] // width):
        start = pl.multiple_of(index_ref[k] * width, width)
        out_ref[:, k * width : (k + 1) * width] = in_ref[:, pl.ds(start, width)]


def reorder(array, index, width, after):
    outs = [shape(array.shape[0], array.shape[1], array.dtype)]
    return call(
        functools.partial(reorder_kernel, width), outs, [index, array], smem=1, after=after
    )[0]


def sums_kernel(count, block, at, index_ref, own_ref, other_ref, grads_ref, *refs):
    outs, chosen = refs[:count], refs[count]
    tokens = own_ref.shape[1]
    for part, out_ref in enumerate(outs):
        blocks = out_ref.shape[0] // block
        for k in range(blocks):
            row = slice(k * block, (k + 1) * block)
            start = pl.multiple_of(index_ref[part * blocks + k] * block, block)
            chosen[row, :tokens] = own_ref[pl.ds(start, block), :]
            chosen[row, tokens:] = other_ref[pl.ds(start, block), :]
        width = out_ref.shape[1]
        out_ref[...] = jnp.dot(
            chosen[...], grads_ref[:, at : at + width], preferred_element_type=F32
        ).astype(out_ref.dtype)
        at += width


def partial_sums(index, own, other, grads, rows, widths, block, kind, after=(), at=0):
    return call(
        functools.partial(sums_kernel, len(widths), block, at),
        [shape(rows, w, kind) for w in widths],
        [index, own, other, grads],
        flops=2 * rows * grads.size,
        vmem=8,
        scratch=[pltpu.VMEM((rows, 2 * own.shape[1]), BF)],
        smem=1,
        after=after,
    )


def halve_kernel(count, *refs):
    kept, got, kept_out, sent = (refs[i * count : (i + 1) * count] for i in range(4))
    for k, g, o, s in zip(kept, got, kept_out, sent):
        rows = o.shape[0]
        s[...] = (k[rows:, :] + g[rows:, :].astype(F32)).astype(s.dtype)
        o[...] = k[:rows, :] + g[:rows, :].astype(F32)


def halve(kept, got, after):
    rows = kept[0].shape[0] // 2
    outs = [shape(rows, k.shape[1], kind) for kind in (F32, BF) for k in kept]
    *result, mark = call(
        with_mark(functools.partial(halve_kernel, len(kept))),
        [*outs, shape(8, 128, F32)],
        [*kept, *got],
        after=after,
    )
    return result[: len(kept)], result[len(kept) :], mark


def adam_kernel(count, *refs):
    kept, got = refs[:count], refs[count : 2 * count]
    first_ref, second_ref = refs[2 * count : 2 * count + 2]
    new_first_ref, new_second_ref = refs[2 * count + 2 : 2 * count + 4]
    directions = refs[2 * count + 4 :]
    at = 0
    for k, g, d in zip(kept, got, directions):
        span = slice(at, at + k.shape[1])
        at += k.shape[1]
        lowrank = k[...] + g[...].astype(F32)
        new_first = 0.9 * first_ref[:, span] + 0.1 * lowrank
        new_second = 0.99 * second_ref[:, span] + 0.01 * lowrank * lowrank
        new_first_ref[:, span] = new_first
        new_second_ref[:, span] = new_second
        d[...] = (new_first / first_fix / (jnp.sqrt(new_second / second_fix) + 1e-08)).astype(
            d.dtype
        )


def adam(kept, got, first, second, after):
    outs = [shape(*first.shape, F32)] * 2 + [shape(*k.shape, BF) for k in kept]
    result = call(
        functools.partial(adam_kernel, len(kept)),
        outs,
        [*kept, *got, first, second],
        after=after,
    )
    return result[0], result[1], result[2:]


def split_kernel(core_ref, first_ref, second_ref, own_ref, other_ref):
    rows, half = first_ref.shape[0], own_ref.shape[1]
    core = core_ref[0]
    own = pl.ds(pl.multiple_of(core * half, half), half)
    other = pl.ds(pl.multiple_of((1 - core) * half, half), half)
    own_ref[:rows, :] = first_ref[:, own]
    own_ref[rows:, :] = second_ref[:, own]
    other_ref[:rows, :] = first_ref[:, other]
    other_ref[rows:, :] = second_ref[:, other]


def merge_kernel(core_ref, own_ref, got_ref, first_ref, second_ref):
    rows = own_ref.shape[0] // 2
    core = core_ref[0]
    own = pl.ds(pl.multiple_of(core * rows, rows), rows)
    other = pl.ds(pl.multiple_of((1 - core) * rows, rows), rows)
    first_ref[own, :] = own_ref[:rows, :]
    first_ref[other, :] = got_ref[:rows, :]
    second_ref[own, :] = own_ref[rows:, :]
    second_ref[other, :] = got_ref[rows:, :]


def pick_kernel(which_ref, first_ref, second_ref, out_ref):
    rows = out_ref.shape[0] // 2
    start = pl.multiple_of(which_ref[0] * rows, rows)
    out_ref[:rows, :] = first_ref[pl.ds(start, rows), :]
    out_ref[rows:, :] = second_ref[pl.ds(start, rows), :]


def join_kernel(core_ref, first_ref, second_ref, other_ref, out_first_ref, out_second_ref):
    rows, half = out_first_ref.shape[0], first_ref.shape[1]
    core = core_ref[0]
    start = pl.multiple_of(core * rows, rows)
    own = pl.ds(pl.multiple_of(core * half, half), half)
    other = pl.ds(pl.multiple_of((1 - core) * half, half), half)
    out_first_ref[:, own] = first_ref[pl.ds(start, rows), :]
    out_first_ref[:, other] = other_ref[:rows, :]
    out_second_ref[:, own] = second_ref[pl.ds(start, rows), :]
    out_second_ref[:, other] = other_ref[rows:, :]


def early_kernel(count, *refs):
    factors, parts, out_ref = refs[:count], refs[count : 2 * count], refs[2 * count]
    at = 0
    for f, p in zip(factors, parts):
        depth, width = p.shape
        out_ref[:, at : at + width] = jnp.dot(
            f[:, :depth], p[...], preferred_element_type=F32
        )
        at += width


def late_kernel(count, row, at, *refs):
    factors, parts, sum_ref, out_ref = (
        refs[:count],
        refs[count : 2 * count],
        refs[2 * count],
        refs[2 * count + 1],
    )
    rows = out_ref.shape[0]
    to = 0
    for f, p in zip(factors, parts):
        depth, width = p.shape
        product = jnp.dot(f[row : row + rows, depth:], p[...], preferred_element_type=F32)
        out_ref[:, to : to + width] = (
            sum_ref[row : row + rows, at : at + width] + product
        ).astype(out_ref.dtype)
        at += width
        to += width


def body(activations, grad_output, projector, first_moment, second_moment):
    place = lax.axis_index("fsdp").astype(jnp.int32)
    tp_place = lax.axis_index("tp").astype(jnp.int32)
    core = place & 1
    chip = place >> 1
    tokens, width = grad_output.shape
    half = width // 2
    rank = projector.shape[1]
    block = rank // 16
    column_count = rank // 8
    wide = half * 5 // 7
    widths = (wide, half - wide)
    rows = first_moment.shape[0]

    def my_half(array):
        return lax.dynamic_slice_in_dim(array, core * half, half, 1)

    def other_half(array):
        return lax.dynamic_slice_in_dim(array, (1 - core) * half, half, 1)

    sum_orders = (([1, 3, 4, 12], [3, 1, 12, 4]), ([4, 12, 1, 3], [12, 4, 3, 1]))
    back_orders = [[o[::-1] for o in orders] for orders in sum_orders]
    ranks = jnp.arange(rank, dtype=jnp.int32)
    rank_tables = []
    for orders in back_orders:
        blocks = chip ^ table(core, [doubled(o) for o in orders])
        rank_tables.append((blocks[:, None] * block + ranks[None, :block]).reshape(-1))

    moments_own, moments_other = call(
        split_kernel,
        [shape(2 * rows, half, F32)] * 2,
        [core[None], first_moment, second_moment],
        smem=1,
    )
    moments_got = swap_core(moments_other)
    projector_other = swap_core(projector)

    grads_got = swap_core(other_half(grad_output))
    order = jnp.array([x + z for x in (0, 2, 4, 6) for z in (0, 8, 16, 24)], jnp.int32)
    index = jnp.concatenate([place ^ order, place ^ 1 ^ order])
    act = reorder(activations, index, projector.shape[0], rank_tables)

    columns = lax.dynamic_slice_in_dim(projector, tp_place * column_count, column_count, 1)
    for masks, after in (((8, 16, 24), ()), ((2, 4, 6), (act, grads_got))):
        got = [swap(columns, "fsdp", (m, m)) for m in masks]
        columns = stack([[columns] + got], after)[0]
    columns_other = swap_core(columns)
    depth = columns.shape[0]
    dims = (((0,), (1,)), ((), ()))
    own = lax.dot_general(columns, act[:, :depth], dims, preferred_element_type=F32)
    own = own + lax.dot_general(columns_other, act[:, depth:], dims, preferred_element_type=F32)
    own = own.astype(BF)

    coords = stack([[own, swap(own, "tp", (1, 1))]])[0]
    coords = stack(
        [[coords] + [swap(coords, "tp", (m, m)) for m in (2, 4, 6)]],
        [moments_got, projector_other],
    )[0]
    coords_other = swap_core(coords)

    grads = jnp.concatenate(
        [my_half(grad_output), grads_got], axis=0
    )
    first, second = call(
        merge_kernel,
        [shape(2 * rows, half, F32)] * 2,
        [core[None], moments_own, moments_got],
        smem=1,
    )
    both = jnp.concatenate([projector, projector_other], axis=0)

    keep_index, send_index = [], []
    for orders in sum_orders:
        wanted = chip ^ table(core, [doubled(o[::-1]) for o in orders])
        position = 2 * (tp_place ^ (wanted >> 1)) + (wanted & 1)
        keep_index.append(position[:8])
        send_index.append(position[8:])
    factors = []
    for wanted in rank_tables:
        choose = (ranks[:, None] == wanted[None, :]).astype(BF)
        factors.append(jnp.dot(both, choose, preferred_element_type=F32).astype(BF))

    def exchange(arrays, orders_of, stage):
        return [
            swap(a, "fsdp", [2 * o[stage] for o in orders]) for a, orders in zip(arrays, orders_of)
        ]

    arrays = (coords, coords_other, grads, rank // 2, widths, block)
    tail = (rank // 2, widths[1:], block, BF)
    sent = partial_sums(send_index[0], *arrays[:3], rank // 2, widths[:1], block, BF)
    sent += partial_sums(send_index[1], *arrays[:3], *tail, after=sent, at=widths[0])
    kept = partial_sums(jnp.concatenate(keep_index), *arrays, F32)
    marks = []
    for stage in range(3):
        kept, sent, mark = halve(kept, exchange(sent, sum_orders, stage), marks)
        marks = [swap_core(mark)]
    got = exchange(sent, sum_orders, 3)
    new_first, new_second, parts = adam(kept, got, first, second, [*factors, *marks])

    states_other = swap_core(
        call(
            pick_kernel,
            [shape(2 * rows, half, F32)],
            [(1 - core)[None], new_first, new_second],
            smem=1,
        )[0]
    )
    out_first, out_second, joined = call(
        with_mark(join_kernel),
        [shape(rows, width, F32)] * 2 + [shape(8, 128, F32)],
        [core[None], new_first, new_second, states_other],
        smem=1,
    )
    marks = [states_other]
    for stage in range(4):
        got = exchange(parts, back_orders, stage)
        if stage == 1:
            marks = [*marks, joined]
        if stage < 3:
            parts, mark = stack_marked([[p, g] for p, g in zip(parts, got)], marks)
            marks = [swap_core(mark)]
    count = len(parts)
    flops = rank * half * both.shape[0]
    early = call(
        functools.partial(early_kernel, count),
        [shape(both.shape[0], half, F32)],
        [*factors, *parts],
        flops=flops,
        vmem=8,
        after=marks,
    )[0]

    def late(row, parts, after=()):
        at = sum(widths[: parts.start])
        span = sum(widths[parts])
        return call(
            functools.partial(late_kernel, len(widths[parts]), row, at),
            [shape(tokens, span, BF)],
            [*factors[parts], *got[parts], early],
            flops=rank * tokens * span,
            after=after,
        )[0]

    every = slice(0, count)
    other = swap_core(late(tokens, every))
    update = by_core(core, late(0, every), other, 1)
    return (out_first, out_second, update)


def solution(mesh):
    return jax.shard_map(
        body,
        mesh=mesh,
        in_specs=(
            P("fsdp", None),
            P("fsdp", "tp"),
            P("fsdp", None),
            P("fsdp", "tp"),
            P("fsdp", "tp"),
        ),
        out_specs=(P("fsdp", "tp"), P("fsdp", "tp"), P("fsdp", "tp")),
        check_vma=False,
    )
```
